512 devices in a mesh: ctx: 64 (over z, y_lo, core), head: 8 (over x, y_hi).
Axes of the slice: x: 4, y: 4 (y_hi: 2, y_lo: 2; y = y_hi * 2 + y_lo), z: 16, core: 2. Of those that a mesh axis runs over, the one named last changes fastest.
Arguments:
- queries: bfloat16 [2, 64, 64, 128], P(None, 'ctx', 'head'), may hold values from -120 to 120
- new_keys: bfloat16 [2, 64, 8, 128], P(None, 'ctx', 'head'), may hold values from -6 to 6
- new_values: bfloat16 [2, 64, 8, 128], P(None, 'ctx', 'head'), may hold values from -6 to 6
- suffix_keys: bfloat16 [64, 512, 8, 128], P('ctx', None, 'head'), may hold values from -6 to 6
- suffix_values: bfloat16 [64, 512, 8, 128], P('ctx', None, 'head'), may hold values from -6 to 6
- suffix_lengths: int32 [64], P('ctx'), may hold values from 1 to 512, 16384 in all
- prefix_keys: bfloat16 [65536, 8, 128], P('ctx', 'head'), may hold values from -6 to 6
- prefix_values: bfloat16 [65536, 8, 128], P('ctx', 'head'), may hold values from -6 to 6
- out_weight: bfloat16 [8192, 5120], P('head', 'ctx'), may hold values from -0.0625 to 0.0625
- residual: bfloat16 [2, 64, 5120], P(None, 'head', 'ctx'), may hold values from -6 to 6
Outputs:
- layer_out: bfloat16 [2, 64, 5120], P(None, 'head', 'ctx')
The draws below stay inside these ranges and needn't reach their ends.
All inputs are finite; a program needn't handle non-finite values. No bound on the sum of `suffix_lengths` on one device may be relied on, other than what follows from the above.
Results may differ from the reference program's by a relative error of at most 0.0068.
Values may be sent and summed in bfloat16 or wider, within the bound.
No kernel may reach another device: no remote copies, remote signals or barrier semaphores. Data moves between devices by JAX's collectives and lax.ppermute only.
A program may use at most 128 MiB of HBM per device.

```python
import math
import jax
import jax.numpy as jnp
import numpy as np
from jax import lax

D = 5120
HEADS = 64
KVH = 8
HD = 128
STEPS = 2
S_MAX = 512
B = 64
PREFIX = 65536


def draw_prefix_keys(key, part):
    key = jax.random.fold_in(key, 3)
    drawn_array = jnp.clip(jax.random.normal(key, (PREFIX, KVH, HD), jnp.float32), -6.0, 6.0)
    return drawn_array.astype(jnp.bfloat16)


def draw_queries(key, part):
    key = jax.random.fold_in(key, 5)
    array_shape = (STEPS, B, HEADS, HD)
    drawn_array = 2.5 * jnp.clip(jax.random.normal(key, array_shape, jnp.float32), -6.0, 6.0)
    return drawn_array.astype(jnp.bfloat16)


def steps_of(key, shape, split, smallest, top_value):
    level, own = 1.0, jax.random.fold_in(key, 6)
    for axis_at, blocks in split:
        draws = jnp.exp(jax.random.uniform(jax.random.fold_in(own, axis_at), (blocks,), jnp.float32, smallest / len(split), top_value / len(split)))
        level = level * jnp.repeat(draws, shape[axis_at] // blocks).reshape([-1 if axis == axis_at else 1 for axis in range(len(shape))])
    return level


def length_profile(count, total, reach, skew):
    portions = [(1 << 20) // math.isqrt(rank ** skew) + 1 for rank in range(2, count + 1)]
    spare, holding = total - reach - (count - 1), [1] * (count - 1)
    while spare > 0:
        movable = [i for i in range(count - 1) if holding[i] < reach]
        pool, budget = sum([portions[i] for i in movable]), spare
        for i in movable:
            more = min(reach - holding[i], max(1, budget * portions[i] // pool), spare)
            holding[i] = holding[i] + more
            spare = spare - more
    return np.array([reach] + holding)


def ragged(stream_key, amount, total, most, slope):
    if amount == 2:
        one = jax.random.randint(stream_key, (), max(1, total - most), min(most, total - 1) + 1)
        return jnp.stack([one, total - one])
    tallies = jnp.asarray(length_profile(amount, total, most, slope), jnp.int32)
    pairs = (amount - 1) // 2
    source_of, taker = tallies[1:1 + 2 * pairs:2], tallies[2:2 + 2 * pairs:2]
    margin = jnp.minimum(source_of - 1, most - taker)
    passed = jax.random.randint(jax.random.fold_in(stream_key, 1), (pairs,), 0, 1 << 20) % (margin + 1)
    tallies = tallies.at[1:1 + 2 * pairs:2].set(source_of - passed).at[2:2 + 2 * pairs:2].set(taker + passed)
    return tallies[jax.random.permutation(jax.random.fold_in(stream_key, 2), amount)]


def bell_draw(rng, extent, deviation, reach, shards=(), held_as=jnp.bfloat16):
    entries = jax.random.normal(rng, extent, jnp.float32) * deviation
    if len(shards) > 0:
        entries = steps_of(rng, extent, shards, -0.22, 0.18) * entries
    return jnp.clip(entries, min=-reach, max=reach).astype(held_as)


def setup_inputs(seed: int = 0) -> dict:
    key_list = jax.random.split(jax.random.key(seed), 11)
    queries = draw_queries(jax.random.fold_in(key_list[10], 71), 0)
    new_keys = bell_draw(key_list[1], (STEPS, B, KVH, HD), 2.0, 6.0, ((1, 64), (2, 8)))
    new_values = bell_draw(key_list[2], (STEPS, B, KVH, HD), 1.0, 6.0, ((1, 64), (2, 8)))
    suffix_keys = bell_draw(key_list[3], (B, S_MAX, KVH, HD), 1.5, 6.0, ((0, 64), (2, 8)))
    suffix_values = bell_draw(key_list[4], (B, S_MAX, KVH, HD), 1.0, 6.0, ((0, 64), (2, 8)))
    suffix_lengths = ragged(key_list[5], B, B * S_MAX // 2, S_MAX, 1).astype(jnp.int32)
    prefix_keys = draw_prefix_keys(jax.random.fold_in(key_list[10], 71), 0)
    prefix_values = bell_draw(key_list[7], (PREFIX, KVH, HD), 1.0, 6.0, ((0, 64), (1, 8)))
    out_weight = bell_draw(key_list[8], (HEADS * HD, D), (HEADS * HD) ** -0.5, 0.0625, ((0, 8), (1, 64)))
    residual = bell_draw(key_list[9], (STEPS, B, D), 0.5, 6.0, ((1, 8), (2, 64)))
    return {"queries": queries, "new_keys": new_keys, "new_values": new_values, "suffix_keys": suffix_keys, "suffix_values": suffix_values, "suffix_lengths": suffix_lengths, "prefix_keys": prefix_keys, "prefix_values": prefix_values, "out_weight": out_weight, "residual": residual}


NEG_FILL = -1e+30

def merge_states(former, latter):
    highest = jnp.maximum(former[1], latter[1])
    factor_a = jnp.exp(former[1] - highest)
    factor_b = jnp.exp(latter[1] - highest)
    weighted = former[0] * factor_a[..., None] + latter[0] * factor_b[..., None]
    return (weighted, highest, former[2] * factor_a + latter[2] * factor_b)

def local_state(query_five, suffix_keys, suffix_values, new_keys, new_values, suffix_lengths):
    scaling = 1.0 / math.sqrt(HD)
    query_wide = query_five.astype(jnp.float32)
    suffix_scores = jnp.einsum('tbkgd,bskd->tbkgs', query_wide, suffix_keys.astype(jnp.float32)) * scaling
    slot_count = suffix_keys.shape[1]
    usable = jnp.arange(slot_count, dtype=jnp.int32)[None, :] < suffix_lengths.astype(jnp.int32)[:, None]
    usable = usable[None, :, None, None, :]
    suffix_scores = jnp.where(usable, suffix_scores, NEG_FILL)
    new_scores = jnp.einsum('tbkgd,ubkd->tbkgu', query_wide, new_keys.astype(jnp.float32)) * scaling
    step_count = new_keys.shape[0]
    causal = jnp.arange(step_count)[None, :] <= jnp.arange(step_count)[:, None]
    causal = causal[:, None, None, None, :]
    new_scores = jnp.where(causal, new_scores, NEG_FILL)
    highest = jnp.maximum(suffix_scores.max(-1), new_scores.max(-1))
    suffix_weights = jnp.where(usable, jnp.exp(suffix_scores - highest[..., None]), 0.0)
    new_weights = jnp.where(causal, jnp.exp(new_scores - highest[..., None]), 0.0)
    weight_sum = suffix_weights.sum(-1) + new_weights.sum(-1)
    weighted = jnp.einsum('tbkgs,bskd->tbkgd', suffix_weights.astype(jnp.bfloat16).astype(jnp.float32), suffix_values.astype(jnp.float32))
    weighted = weighted + jnp.einsum('tbkgu,ubkd->tbkgd', new_weights.astype(jnp.bfloat16).astype(jnp.float32), new_values.astype(jnp.float32))
    return (weighted, highest, weight_sum)

def prefix_state(query_five, keys, values, carried):
    scaling = 1.0 / math.sqrt(HD)
    block_width = math.gcd(keys.shape[0], 8192)
    block_count = keys.shape[0] // block_width
    key_blocks = keys.reshape(block_count, block_width, keys.shape[1], keys.shape[2])
    value_blocks = values.reshape(block_count, block_width, values.shape[1], values.shape[2])
    query_wide = query_five.astype(jnp.float32)

    def one_block(running, blocks):
        key_block, value_block = blocks
        weighted, run_max, weight_sum = running
        scores = jnp.einsum('sbkgd,nkd->sbkgn', query_wide, key_block.astype(jnp.float32)) * scaling
        highest = jnp.maximum(run_max, scores.max(-1))
        factor = jnp.exp(run_max - highest)
        weights = jnp.exp(scores - highest[..., None])
        weight_sum = weight_sum * factor + weights.sum(-1)
        weighted = weighted * factor[..., None] + jnp.einsum('sbkgn,nkd->sbkgd', weights.astype(jnp.bfloat16).astype(jnp.float32), value_block.astype(jnp.float32))
        return ((weighted, highest, weight_sum), None)
    finished, _ = lax.scan(one_block, carried, (key_blocks, value_blocks))
    return finished

def reference(queries, new_keys, new_values, suffix_keys, suffix_values, suffix_lengths, prefix_keys, prefix_values, out_weight, residual):
    group = HEADS // KVH
    query_all = queries.reshape(STEPS, B, KVH, group, HD)
    pieces = []
    for kv_index in range(KVH):
        query_five = query_all[:, :, kv_index:kv_index + 1]
        carried = local_state(query_five, suffix_keys[:, :, kv_index:kv_index + 1], suffix_values[:, :, kv_index:kv_index + 1], new_keys[:, :, kv_index:kv_index + 1], new_values[:, :, kv_index:kv_index + 1], suffix_lengths)
        carried = prefix_state(query_five, prefix_keys[:, kv_index:kv_index + 1], prefix_values[:, kv_index:kv_index + 1], carried)
        pieces.append(carried[0] / carried[2][..., None])
    attended = jnp.concatenate(pieces, axis=2).reshape(STEPS, B, HEADS, HD).astype(jnp.bfloat16)
    projected = jnp.dot(attended.reshape(STEPS * B, HEADS * HD), out_weight, preferred_element_type=jnp.float32)
    return (projected.reshape(STEPS, B, D) + residual.astype(jnp.float32)).astype(jnp.bfloat16)
```

```python
import functools
import math

import jax
import jax.numpy as jnp
from jax import lax
from jax.experimental import pallas as pl
from jax.experimental.pallas import tpu as pltpu
from jax.sharding import PartitionSpec as P

NEG_FILL = -1e30
BF16, F32 = jnp.bfloat16, jnp.float32
SCALE = math.log2(math.e) / math.sqrt(128)
NT = (((1,), (1,)), ((), ()))
STAT_ROWS = 8


def split_three(x):
    high = x.astype(BF16).astype(F32)
    rest = x - high
    middle = rest.astype(BF16).astype(F32)
    return [high, middle, rest - middle]


def prefix_kernel(q_ref, k0_ref, k1_ref, v0_ref, v1_ref, out_ref):
    key_block, row_block = 256, 256
    blocks = k0_ref.shape[0] // key_block
    for at in range(q_ref.shape[0] // row_block):
        q = q_ref[at * row_block : (at + 1) * row_block, :]
        scores = [
            lax.dot_general(k_ref[i * key_block : (i + 1) * key_block, :], q, NT, preferred_element_type=F32)
            for k_ref in (k0_ref, k1_ref)
            for i in range(blocks)
        ]
        highest = functools.reduce(jnp.maximum, [s.max(0, keepdims=True) for s in scores])
        total = jnp.zeros_like(highest)
        weighted = jnp.zeros((128, row_block), F32)
        values = [v_ref[i * key_block : (i + 1) * key_block, :] for v_ref in (v0_ref, v1_ref) for i in range(blocks)]
        for s, v in zip(scores, values):
            p = jnp.exp2((s - highest) * SCALE)
            total = total + p.sum(0, keepdims=True)
            weighted = weighted + lax.dot_general(
                v, p.astype(BF16), (((0,), (0,)), ((), ())), preferred_element_type=F32
            )
        first, count = at * row_block // 16, row_block // 16
        out_ref[first : first + count, 0:16, :] = weighted.T.astype(BF16).reshape(count, 16, 128)
        zero = jnp.zeros_like(highest)
        stats = jnp.concatenate(split_three(highest) + split_three(total) + [zero, zero], 0).astype(BF16)
        for part in range(row_block // 128):
            piece = stats[:, part * 128 : (part + 1) * 128]
            out_ref[first + part * 8 : first + part * 8 + 8, 16:24, :] = jnp.broadcast_to(piece[None], (8, 8, 128))


def suffix_kernel(length_ref, q_ref, sk_ref, sv_ref, nk_ref, nv_ref, o_ref, m_ref, l_ref):
    q = q_ref[...]
    s = lax.dot_general(q, sk_ref[...], NT, preferred_element_type=F32)
    usable = lax.broadcasted_iota(jnp.int32, s.shape, 1) < length_ref[0]
    s = jnp.where(usable, s, NEG_FILL)
    q_wide = q.astype(F32)
    new_keys, new_values = nk_ref[...].astype(F32), nv_ref[...].astype(F32)
    rows = q.shape[0]
    second = lax.broadcasted_iota(jnp.int32, (rows, 1), 0) >= rows // 2
    n0 = (q_wide * new_keys[0:1]).sum(1, keepdims=True)
    n1 = jnp.where(second, (q_wide * new_keys[1:2]).sum(1, keepdims=True), NEG_FILL)
    highest = jnp.maximum(s.max(1, keepdims=True), jnp.maximum(n0, n1))
    p = jnp.where(usable, jnp.exp2((s - highest) * SCALE), 0.0)
    p0 = jnp.exp2((n0 - highest) * SCALE)
    p1 = jnp.where(second, jnp.exp2((n1 - highest) * SCALE), 0.0)
    weighted = jnp.dot(p.astype(BF16), sv_ref[...], preferred_element_type=F32)
    weighted = weighted + p0.astype(BF16).astype(F32) * new_values[0:1] + p1.astype(BF16).astype(F32) * new_values[1:2]
    o_ref[...] = weighted
    m_ref[...] = jnp.broadcast_to(highest, m_ref.shape)
    l_ref[...] = jnp.broadcast_to(p.sum(1, keepdims=True) + p0 + p1, l_ref.shape)


def combine_kernel(place_ref, got_ref, so_ref, sm_ref, sl_ref, out_ref, turned):
    sources = got_ref.shape[0]
    stats = got_ref[:, 16:24, :].astype(F32)
    highest = stats[:, 0, :] + (stats[:, 1, :] + stats[:, 2, :])
    total = stats[:, 3, :] + (stats[:, 4, :] + stats[:, 5, :])
    rest = jnp.zeros((128 - 2 * sources, 128), F32)
    turned[...] = jnp.concatenate([highest, total, rest], 0).T
    mine = turned[pl.ds(pl.multiple_of(place_ref[0] * 16, 16), 16), :]
    maxima, totals = mine[:, 0:sources], mine[:, sources : 2 * sources]
    own_max, own_total = sm_ref[:, 0:1], sl_ref[:, 0:1]
    top = jnp.maximum(maxima.max(1, keepdims=True), own_max)
    factor = jnp.exp2((maxima - top) * SCALE)
    own_factor = jnp.exp2((own_max - top) * SCALE)
    weight_total = (factor * totals).sum(1, keepdims=True) + own_factor * own_total
    weighted = own_factor * so_ref[...]
    for i in range(sources):
        weighted = weighted + factor[:, i : i + 1] * got_ref[i, 0:16, :].astype(F32)
    out_ref[...] = (weighted / weight_total).astype(BF16)


def vmem(n):
    return [pl.BlockSpec(memory_space=pltpu.VMEM)] * n


SMEM = pl.BlockSpec(memory_space=pltpu.SMEM)
PARAMS = pltpu.CompilerParams(vmem_limit_bytes=32 * 1024 * 1024)


def body(
    queries,
    new_keys,
    new_values,
    suffix_keys,
    suffix_values,
    suffix_lengths,
    prefix_keys,
    prefix_values,
    out_weight,
    residual,
):
    steps, _, group, hd = queries.shape
    rows = steps * group
    ctx = lax.axis_size("ctx")
    heads = lax.axis_size("head")
    half = ctx // 2
    same_core = [[2 * i + core for i in range(half)] for core in range(2)]
    pairs = [[2 * i, 2 * i + 1] for i in range(half)]
    swap = [(i, i ^ 1) for i in range(ctx)]

    def spread(x):
        copies = jnp.broadcast_to(x[None], (half,) + x.shape)
        return lax.all_to_all(copies, "ctx", 0, 0, axis_index_groups=same_core, tiled=True)

    query_rows = queries.reshape(rows, hd)
    keys, values = prefix_keys.reshape(-1, hd), prefix_values.reshape(-1, hd)
    other_keys = lax.ppermute(keys, "ctx", swap)
    other_values = lax.ppermute(values, "ctx", swap)
    class_queries = spread(query_rows).reshape(half * rows, hd)

    own = pl.pallas_call(
        suffix_kernel,
        out_shape=[jax.ShapeDtypeStruct((rows, hd), F32)] * 3,
        in_specs=[SMEM] + vmem(5),
        out_specs=vmem(3),
        compiler_params=PARAMS,
        name="suffix_state",
    )(
        suffix_lengths,
        query_rows,
        suffix_keys.reshape(-1, hd),
        suffix_values.reshape(-1, hd),
        new_keys.reshape(-1, hd),
        new_values.reshape(-1, hd),
    )

    partial = pl.pallas_call(
        prefix_kernel,
        out_shape=jax.ShapeDtypeStruct((half, rows + STAT_ROWS, hd), BF16),
        in_specs=vmem(5),
        out_specs=vmem(1)[0],
        compiler_params=PARAMS,
        name="prefix_state",
    )(class_queries, keys, other_keys, values, other_values)
    received = lax.all_to_all(partial, "ctx", 0, 0, axis_index_groups=same_core, tiled=True)

    place = (lax.axis_index("ctx") // 2) % 8
    attended = pl.pallas_call(
        combine_kernel,
        out_shape=jax.ShapeDtypeStruct((rows, hd), BF16),
        in_specs=[SMEM] + vmem(4),
        out_specs=vmem(1)[0],
        scratch_shapes=[pltpu.VMEM((128, 128), F32)],
        compiler_params=PARAMS,
        name="combine",
    )(place.astype(jnp.int32).reshape(1), received, *own)

    class_rows = spread(attended)
    every = lax.all_gather(class_rows, "ctx", axis=0, axis_index_groups=pairs)
    every = every.reshape(2, half, steps, group, hd)
    weight = out_weight.reshape(group, hd, -1)
    product = jnp.einsum("citgd,gdn->citn", every, weight, preferred_element_type=F32)
    product = product.reshape(2, heads, half // heads, steps, -1).transpose(1, 3, 2, 0, 4)
    product = product.reshape(heads, steps, ctx // heads, -1)
    terms = lax.all_to_all(product, "head", 0, 0, tiled=True)
    return (terms.sum(0) + residual.astype(F32)).astype(BF16)


def solution(mesh):
    in_specs = (
        P(None, "ctx", "head", None),
        P(None, "ctx", "head", None),
        P(None, "ctx", "head", None),
        P("ctx", None, "head", None),
        P("ctx", None, "head", None),
        P("ctx"),
        P("ctx", "head", None),
        P("ctx", "head", None),
        P("head", "ctx"),
        P(None, "head", "ctx"),
    )
    out_specs = P(None, "head", "ctx")
    return jax.shard_map(body, mesh=mesh, in_specs=in_specs, out_specs=out_specs, check_vma=False)
```

```python
import functools
import math

import jax
import jax.numpy as jnp
from jax import lax
from jax.experimental import pallas as pl
from jax.experimental.pallas import tpu as pltpu
from jax.sharding import PartitionSpec as P

NEG_FILL = -1e30
BF16, F32 = jnp.bfloat16, jnp.float32
SCALE = math.log2(math.e) / math.sqrt(128)
NT = (((1,), (1,)), ((), ()))


def split_three(x):
    high = x.astype(BF16).astype(F32)
    rest = x - high
    middle = rest.astype(BF16).astype(F32)
    return [high, middle, rest - middle]


def sample_rows(parts, count):
    lanes = 16 * count
    sample = lax.broadcasted_iota(jnp.int32, (count, lanes), 0)
    mine = sample == lax.broadcasted_iota(jnp.int32, (count, lanes), 1) // 16
    stacked = jnp.concatenate([jnp.where(mine, part, 0.0) for part in parts], 0).astype(BF16)
    place = lax.broadcasted_iota(jnp.int32, (lanes, 128), 0) % 16
    fold = (place == lax.broadcasted_iota(jnp.int32, (lanes, 128), 1) % 16).astype(F32).astype(BF16)
    folded = jnp.dot(stacked, fold, preferred_element_type=F32)
    lane_part = lax.broadcasted_iota(jnp.int32, (count, 128), 1) // 16
    rows = jnp.zeros((count, 128), F32)
    for p in range(len(parts)):
        rows = jnp.where(lane_part == p, folded[p * count : (p + 1) * count], rows)
    return rows


def prefix_kernel(q_ref, k_ref, v_ref, out_ref):
    key_block, row_block = 256, 256
    starts = [(c, i * key_block) for c in range(k_ref.shape[0]) for i in range(k_ref.shape[1] // key_block)]
    for at in range(q_ref.shape[0] // row_block):
        q = q_ref[at * row_block : (at + 1) * row_block, :]
        scores = [
            lax.dot_general(k_ref[c, i : i + key_block, :], q, NT, preferred_element_type=F32) for c, i in starts
        ]
        highest = functools.reduce(jnp.maximum, [s.max(0, keepdims=True) for s in scores])
        total = jnp.zeros_like(highest)
        weighted = jnp.zeros((128, row_block), F32)
        for s, (c, i) in zip(scores, starts):
            p = jnp.exp2((s - highest) * SCALE)
            total = total + p.sum(0, keepdims=True)
            weighted = weighted + lax.dot_general(
                v_ref[c, i : i + key_block, :], p.astype(BF16), (((0,), (0,)), ((), ())), preferred_element_type=F32
            )
        first, count = at * row_block // 16, row_block // 16
        out_ref[first : first + count, 0:8] = weighted.T.astype(BF16).reshape(count, 8, 2, 128)
        rows = sample_rows(split_three(highest) + split_three(total), count).astype(BF16)
        out_ref[first : first + count, 8] = jnp.broadcast_to(rows[:, None, :], (count, 2, 128))


def suffix_kernel(length_ref, q_ref, sk_ref, sv_ref, nk_ref, nv_ref, o_ref, m_ref, l_ref):
    q = q_ref[...]
    s = lax.dot_general(q, sk_ref[...], NT, preferred_element_type=F32)
    usable = lax.broadcasted_iota(jnp.int32, s.shape, 1) < length_ref[0]
    s = jnp.where(usable, s, NEG_FILL)
    q_wide = q.astype(F32)
    new_keys, new_values = nk_ref[...].astype(F32), nv_ref[...].astype(F32)
    rows = q.shape[0]
    second = lax.broadcasted_iota(jnp.int32, (rows, 1), 0) >= rows // 2
    n0 = (q_wide * new_keys[0:1]).sum(1, keepdims=True)
    n1 = jnp.where(second, (q_wide * new_keys[1:2]).sum(1, keepdims=True), NEG_FILL)
    highest = jnp.maximum(s.max(1, keepdims=True), jnp.maximum(n0, n1))
    p = jnp.where(usable, jnp.exp2((s - highest) * SCALE), 0.0)
    p0 = jnp.exp2((n0 - highest) * SCALE)
    p1 = jnp.where(second, jnp.exp2((n1 - highest) * SCALE), 0.0)
    weighted = jnp.dot(p.astype(BF16), sv_ref[...], preferred_element_type=F32)
    weighted = weighted + p0.astype(BF16).astype(F32) * new_values[0:1] + p1.astype(BF16).astype(F32) * new_values[1:2]
    o_ref[...] = weighted
    m_ref[...] = jnp.broadcast_to(highest, m_ref.shape)
    l_ref[...] = jnp.broadcast_to(p.sum(1, keepdims=True) + p0 + p1, l_ref.shape)


def combine_kernel(got_ref, so_ref, sm_ref, sl_ref, out_ref):
    sources = got_ref.shape[0]
    stats = got_ref[:, 8].astype(F32)[:, 0, :]
    parts = jnp.concatenate([stats, jnp.zeros((128 - sources, 128), F32)], 0).T[:, 0:sources]
    maxima = parts[0:16] + (parts[16:32] + parts[32:48])
    totals = parts[48:64] + (parts[64:80] + parts[80:96])
    own_max, own_total = sm_ref[:, 0:1], sl_ref[:, 0:1]
    top = jnp.maximum(maxima.max(1, keepdims=True), own_max)
    factor = jnp.exp2((maxima - top) * SCALE)
    own_factor = jnp.exp2((own_max - top) * SCALE)
    weight_total = (factor * totals).sum(1, keepdims=True) + own_factor * own_total
    weighted = own_factor * so_ref[...]
    for i in range(sources):
        weighted = weighted + factor[:, i : i + 1] * got_ref[i, 0:8].astype(F32).reshape(16, 128)
    attended = (weighted / weight_total).astype(BF16)
    out_ref[...] = jnp.broadcast_to(attended[None], out_ref.shape)


def project_kernel(place_ref, x_ref, w_ref, far_ref, out_ref):
    samples, rows, hd = x_ref.shape
    group = w_ref.shape[2] // hd
    heads = out_ref.shape[1]
    x = x_ref[...].astype(F32).reshape(samples * rows // group, group, hd)
    x = jnp.swapaxes(x, 0, 1).astype(BF16)
    side = place_ref[0] // 2 * 2
    for ref, at in ((w_ref, side), (far_ref, 2 - side)):
        for core in range(2):
            y = functools.reduce(
                jnp.add,
                [
                    lax.dot_general(
                        x[g], ref[core, :, g * hd : (g + 1) * hd], NT, preferred_element_type=F32
                    )
                    for g in range(group)
                ],
            )
            out_ref[at + core] = y.reshape(heads, -1, y.shape[1])


def finish_kernel(terms_ref, residual_ref, out_ref):
    planes, heads = terms_ref.shape[:2]
    steps = residual_ref.shape[0]
    sums = [functools.reduce(jnp.add, [terms_ref[d, h] for h in range(heads)]) for d in range(planes)]
    for t in range(steps):
        rows = [sums[d][z * steps + t][None] for z in range(sums[0].shape[0] // steps) for d in range(planes)]
        out_ref[t] = (jnp.concatenate(rows, 0) + residual_ref[t].astype(F32)).astype(BF16)


def vmem(n):
    return [pl.BlockSpec(memory_space=pltpu.VMEM)] * n


SMEM = pl.BlockSpec(memory_space=pltpu.SMEM)
PARAMS = pltpu.CompilerParams(vmem_limit_bytes=32 * 1024 * 1024)


def body(
    queries,
    new_keys,
    new_values,
    suffix_keys,
    suffix_values,
    suffix_lengths,
    prefix_keys,
    prefix_values,
    out_weight,
    residual,
):
    steps, _, group, hd = queries.shape
    rows = steps * group
    ctx = lax.axis_size("ctx")
    heads = lax.axis_size("head")
    depth = ctx // 4
    lines = [[4 * z + j for z in range(depth)] for j in range(4)]
    halves = [[2 * i + core for i in range(ctx // 2)] for core in range(2)]
    pairs = [[2 * i, 2 * i + 1] for i in range(ctx // 2)]
    planes = [[(4 * z + j) * heads + h for j in range(4) for h in range(heads)] for z in range(depth)]
    place = lax.axis_index("ctx").astype(jnp.int32)

    def swap(x, bit):
        return lax.ppermute(x, "ctx", [(i, i ^ bit) for i in range(ctx)])

    def exchange(x, groups):
        return lax.all_to_all(x, "ctx", 0, 0, axis_index_groups=groups, tiled=True)

    def both(x):
        return lax.all_gather(x, "ctx", axis=0, axis_index_groups=pairs)

    query_rows = queries.reshape(rows, hd)
    keys, values = both(prefix_keys.reshape(-1, hd)), both(prefix_values.reshape(-1, hd))
    copies = jnp.broadcast_to(query_rows[None], (ctx // 2, rows, hd))
    half_queries = exchange(copies, halves).reshape(ctx // 2 * rows, hd)

    own = pl.pallas_call(
        suffix_kernel,
        out_shape=[jax.ShapeDtypeStruct((rows, hd), F32)] * 3,
        in_specs=[SMEM] + vmem(5),
        out_specs=vmem(3),
        compiler_params=PARAMS,
        name="suffix_state",
    )(
        suffix_lengths,
        query_rows,
        suffix_keys.reshape(-1, hd),
        suffix_values.reshape(-1, hd),
        new_keys.reshape(-1, hd),
        new_values.reshape(-1, hd),
    )

    partial = pl.pallas_call(
        prefix_kernel,
        out_shape=jax.ShapeDtypeStruct((ctx // 2, rows // 2 + 1, 2, hd), BF16),
        in_specs=vmem(3),
        out_specs=vmem(1)[0],
        compiler_params=PARAMS,
        name="prefix_state",
    )(half_queries, keys, values)
    received = exchange(partial, halves)

    weight = out_weight.T
    far_weight = swap(weight, 2)
    weights, far_weights = both(weight), both(far_weight)

    attended = pl.pallas_call(
        combine_kernel,
        out_shape=jax.ShapeDtypeStruct((depth, rows, hd), BF16),
        in_specs=vmem(4),
        out_specs=vmem(1)[0],
        compiler_params=PARAMS,
        name="combine",
    )(received, *own)

    line_rows = exchange(attended, lines)
    columns = weight.shape[0]
    product = pl.pallas_call(
        project_kernel,
        out_shape=jax.ShapeDtypeStruct((4, heads, depth * steps // heads, columns), F32),
        in_specs=[SMEM] + vmem(3),
        out_specs=vmem(1)[0],
        compiler_params=PARAMS,
        name="project",
    )((place % 4).reshape(1), line_rows, weights, far_weights)
    product = product.reshape(4 * heads, depth * steps // heads, columns)
    terms = lax.all_to_all(product, ("ctx", "head"), 0, 0, axis_index_groups=planes, tiled=True)
    return pl.pallas_call(
        finish_kernel,
        out_shape=jax.ShapeDtypeStruct(residual.shape, BF16),
        in_specs=vmem(2),
        out_specs=vmem(1)[0],
        compiler_params=PARAMS,
        name="finish",
    )(terms.reshape(4, heads, depth * steps // heads, columns), residual)


def solution(mesh):
    in_specs = (
        P(None, "ctx", "head", None),
        P(None, "ctx", "head", None),
        P(None, "ctx", "head", None),
        P("ctx", None, "head", None),
        P("ctx", None, "head", None),
        P("ctx"),
        P("ctx", "head", None),
        P("ctx", "head", None),
        P("head", "ctx"),
        P(None, "head", "ctx"),
    )
    out_specs = P(None, "head", "ctx")
    return jax.shard_map(body, mesh=mesh, in_specs=in_specs, out_specs=out_specs, check_vma=False)
```

```python
import functools
import math

import jax
import jax.numpy as jnp
from jax import lax
from jax.experimental import pallas as pl
from jax.experimental.pallas import tpu as pltpu
from jax.sharding import PartitionSpec as P

NEG_FILL = -1e30
BF16, F32 = jnp.bfloat16, jnp.float32
SCALE = math.log2(math.e) / math.sqrt(128)
NT = (((1,), (1,)), ((), ()))


def split_three(x):
    high = x.astype(BF16).astype(F32)
    rest = x - high
    middle = rest.astype(BF16).astype(F32)
    return [high, middle, rest - middle]


def sample_rows(parts, count):
    lanes = 16 * count
    sample = lax.broadcasted_iota(jnp.int32, (count, lanes), 0)
    mine = sample == lax.broadcasted_iota(jnp.int32, (count, lanes), 1) // 16
    stacked = jnp.concatenate([jnp.where(mine, part, 0.0) for part in parts], 0).astype(BF16)
    place = lax.broadcasted_iota(jnp.int32, (lanes, 128), 0) % 16
    fold = (place == lax.broadcasted_iota(jnp.int32, (lanes, 128), 1) % 16).astype(F32).astype(BF16)
    folded = jnp.dot(stacked, fold, preferred_element_type=F32)
    lane_part = lax.broadcasted_iota(jnp.int32, (count, 128), 1) // 16
    rows = jnp.zeros((count, 128), F32)
    for p in range(len(parts)):
        rows = jnp.where(lane_part == p, folded[p * count : (p + 1) * count], rows)
    return rows


def prefix_kernel(q_ref, kv_ref, near_ref, fk_ref, fv_ref, out_ref):
    key_block, row_block = 256, 256
    depth = kv_ref.shape[0] // 2
    starts = range(0, depth, key_block)
    shards = [
        (kv_ref.at[0:depth], kv_ref.at[depth : 2 * depth]),
        (near_ref.at[0:depth], near_ref.at[depth : 2 * depth]),
        (fk_ref.at[0], fv_ref.at[0]),
        (fk_ref.at[1], fv_ref.at[1]),
    ]
    for at in range(q_ref.shape[0] // row_block):
        q = q_ref[at * row_block : (at + 1) * row_block, :]
        scores = [
            lax.dot_general(q, k[i : i + key_block, :], NT, preferred_element_type=F32) for k, _ in shards for i in starts
        ]
        values = [v[i : i + key_block, :] for _, v in shards for i in starts]
        highest = functools.reduce(jnp.maximum, scores).max(1, keepdims=True)
        totals, weighted = [], []
        for s, v in zip(scores, values):
            p = jnp.exp2((s - highest) * SCALE)
            totals.append(p)
            weighted.append(jnp.dot(p.astype(BF16), v, preferred_element_type=F32))
        total = functools.reduce(jnp.add, totals).sum(1, keepdims=True)
        weighted = functools.reduce(jnp.add, weighted)
        first, count = at * row_block // 16, row_block // 16
        out_ref[first : first + count, 0:8] = weighted.astype(BF16).reshape(count, 8, 2, 128)
        lane = lax.broadcasted_iota(jnp.int32, (row_block, 128), 1)
        stats = jnp.zeros((row_block, 128), F32)
        parts = split_three(highest) + split_three(total)
        for p, part in enumerate(parts):
            stats = jnp.where(lane == p, part, stats)
        stats = stats.T
        rows = sample_rows([stats[p : p + 1] for p in range(len(parts))], count).astype(BF16)
        out_ref[first : first + count, 8] = jnp.broadcast_to(rows[:, None, :], (count, 2, 128))


def suffix_kernel(length_ref, q_ref, sk_ref, sv_ref, nk_ref, nv_ref, o_ref, m_ref, l_ref):
    q = q_ref[...]
    s = lax.dot_general(q, sk_ref[...], NT, preferred_element_type=F32)
    usable = lax.broadcasted_iota(jnp.int32, s.shape, 1) < length_ref[0]
    s = jnp.where(usable, s, NEG_FILL)
    q_wide = q.astype(F32)
    new_keys, new_values = nk_ref[...].astype(F32), nv_ref[...].astype(F32)
    rows = q.shape[0]
    second = lax.broadcasted_iota(jnp.int32, (rows, 1), 0) >= rows // 2
    n0 = (q_wide * new_keys[0:1]).sum(1, keepdims=True)
    n1 = jnp.where(second, (q_wide * new_keys[1:2]).sum(1, keepdims=True), NEG_FILL)
    highest = jnp.maximum(s.max(1, keepdims=True), jnp.maximum(n0, n1))
    p = jnp.where(usable, jnp.exp2((s - highest) * SCALE), 0.0)
    p0 = jnp.exp2((n0 - highest) * SCALE)
    p1 = jnp.where(second, jnp.exp2((n1 - highest) * SCALE), 0.0)
    weighted = jnp.dot(p.astype(BF16), sv_ref[...], preferred_element_type=F32)
    weighted = weighted + p0.astype(BF16).astype(F32) * new_values[0:1] + p1.astype(BF16).astype(F32) * new_values[1:2]
    o_ref[...] = weighted
    m_ref[...] = jnp.broadcast_to(highest, m_ref.shape)
    l_ref[...] = jnp.broadcast_to(p.sum(1, keepdims=True) + p0 + p1, l_ref.shape)


def combine_kernel(got_ref, so_ref, sm_ref, sl_ref, out_ref):
    sources = got_ref.shape[0]
    stats = got_ref[:, 8].astype(F32)[:, 0, :]
    parts = jnp.concatenate([stats, jnp.zeros((128 - sources, 128), F32)], 0).T[:, 0:sources]
    maxima = parts[0:16] + (parts[16:32] + parts[32:48])
    totals = parts[48:64] + (parts[64:80] + parts[80:96])
    own_max, own_total = sm_ref[:, 0:1], sl_ref[:, 0:1]
    top = jnp.maximum(maxima.max(1, keepdims=True), own_max)
    factor = jnp.exp2((maxima - top) * SCALE)
    own_factor = jnp.exp2((own_max - top) * SCALE)
    weight_total = (factor * totals).sum(1, keepdims=True) + own_factor * own_total
    weighted = own_factor * so_ref[...]
    for i in range(sources):
        weighted = weighted + factor[:, i : i + 1] * got_ref[i, 0:8].astype(F32).reshape(16, 128)
    attended = (weighted / weight_total).astype(BF16)
    out_ref[...] = jnp.broadcast_to(attended[None], out_ref.shape)


def project_kernel(place_ref, x_ref, w_ref, far_ref, out_ref):
    samples, rows, hd = x_ref.shape
    group = w_ref.shape[2] // hd
    heads = out_ref.shape[1]
    x = x_ref[...].astype(F32).reshape(samples * rows // group, group, hd)
    x = jnp.swapaxes(x, 0, 1).astype(BF16)
    side = place_ref[0] // 2 * 2
    for ref, at in ((w_ref, side), (far_ref, 2 - side)):
        for core in range(2):
            y = functools.reduce(
                jnp.add,
                [
                    lax.dot_general(
                        x[g], ref[core, :, g * hd : (g + 1) * hd], NT, preferred_element_type=F32
                    )
                    for g in range(group)
                ],
            )
            out_ref[at + core] = y.reshape(heads, -1, y.shape[1])


def finish_kernel(terms_ref, residual_ref, out_ref):
    planes, heads = terms_ref.shape[:2]
    steps = residual_ref.shape[0]
    sums = [functools.reduce(jnp.add, [terms_ref[d, h] for h in range(heads)]) for d in range(planes)]
    for t in range(steps):
        rows = [sums[d][z * steps + t][None] for z in range(sums[0].shape[0] // steps) for d in range(planes)]
        out_ref[t] = (jnp.concatenate(rows, 0) + residual_ref[t].astype(F32)).astype(BF16)


def vmem(n):
    return [pl.BlockSpec(memory_space=pltpu.VMEM)] * n


SMEM = pl.BlockSpec(memory_space=pltpu.SMEM)
PARAMS = pltpu.CompilerParams(vmem_limit_bytes=32 * 1024 * 1024)


def body(
    queries,
    new_keys,
    new_values,
    suffix_keys,
    suffix_values,
    suffix_lengths,
    prefix_keys,
    prefix_values,
    out_weight,
    residual,
):
    steps, _, group, hd = queries.shape
    rows = steps * group
    ctx = lax.axis_size("ctx")
    heads = lax.axis_size("head")
    depth = ctx // 4
    lines = [[4 * z + j for z in range(depth)] for j in range(4)]
    halves = [[2 * i + core for i in range(ctx // 2)] for core in range(2)]
    pairs = [[2 * i, 2 * i + 1] for i in range(ctx // 2)]
    planes = [[(4 * z + j) * heads + h for j in range(4) for h in range(heads)] for z in range(depth)]
    place = lax.axis_index("ctx").astype(jnp.int32)

    def swap(x, bit):
        return lax.ppermute(x, "ctx", [(i, i ^ bit) for i in range(ctx)])

    def exchange(x, groups):
        return lax.all_to_all(x, "ctx", 0, 0, axis_index_groups=groups, tiled=True)

    def both(x):
        return lax.all_gather(x, "ctx", axis=0, axis_index_groups=pairs)

    query_rows = queries.reshape(rows, hd)
    kv = jnp.concatenate([prefix_keys.reshape(-1, hd), prefix_values.reshape(-1, hd)], 0)
    far = swap(kv, 2)
    near = swap(kv, 1)
    copies = jnp.broadcast_to(query_rows[None], (depth, rows, hd))
    line_queries = exchange(copies, lines).reshape(depth * rows, hd)
    half = kv.shape[0] // 2
    far_keys, far_values = both(far[:half]), both(far[half:])

    own = pl.pallas_call(
        suffix_kernel,
        out_shape=[jax.ShapeDtypeStruct((rows, hd), F32)] * 3,
        in_specs=[SMEM] + vmem(5),
        out_specs=vmem(3),
        compiler_params=PARAMS,
        name="suffix_state",
    )(
        suffix_lengths,
        query_rows,
        suffix_keys.reshape(-1, hd),
        suffix_values.reshape(-1, hd),
        new_keys.reshape(-1, hd),
        new_values.reshape(-1, hd),
    )

    partial = pl.pallas_call(
        prefix_kernel,
        out_shape=jax.ShapeDtypeStruct((depth, rows // 2 + 1, 2, hd), BF16),
        in_specs=vmem(5),
        out_specs=vmem(1)[0],
        compiler_params=PARAMS,
        name="prefix_state",
    )(line_queries, kv, near, far_keys, far_values)
    received = exchange(partial, lines)

    weight = out_weight.T
    far_weight = swap(weight, 2)
    weights, far_weights = both(weight), both(far_weight)

    attended = pl.pallas_call(
        combine_kernel,
        out_shape=jax.ShapeDtypeStruct((depth, rows, hd), BF16),
        in_specs=vmem(4),
        out_specs=vmem(1)[0],
        compiler_params=PARAMS,
        name="combine",
    )(received, *own)

    line_rows = exchange(attended, lines)
    columns = weight.shape[0]
    product = pl.pallas_call(
        project_kernel,
        out_shape=jax.ShapeDtypeStruct((4, heads, depth * steps // heads, columns), F32),
        in_specs=[SMEM] + vmem(3),
        out_specs=vmem(1)[0],
        compiler_params=PARAMS,
        name="project",
    )((place % 4).reshape(1), line_rows, weights, far_weights)
    product = product.reshape(4 * heads, depth * steps // heads, columns)
    terms = lax.all_to_all(product, ("ctx", "head"), 0, 0, axis_index_groups=planes, tiled=True)
    return pl.pallas_call(
        finish_kernel,
        out_shape=jax.ShapeDtypeStruct(residual.shape, BF16),
        in_specs=vmem(2),
        out_specs=vmem(1)[0],
        compiler_params=PARAMS,
        name="finish",
    )(terms.reshape(4, heads, depth * steps // heads, columns), residual)


def solution(mesh):
    in_specs = (
        P(None, "ctx", "head", None),
        P(None, "ctx", "head", None),
        P(None, "ctx", "head", None),
        P("ctx", None, "head", None),
        P("ctx", None, "head", None),
        P("ctx"),
        P("ctx", "head", None),
        P("ctx", "head", None),
        P("head", "ctx"),
        P(None, "head", "ctx"),
    )
    out_specs = P(None, "head", "ctx")
    return jax.shard_map(body, mesh=mesh, in_specs=in_specs, out_specs=out_specs, check_vma=False)
```

```python
import functools
import math

import jax
import jax.numpy as jnp
from jax import lax
from jax.experimental import pallas as pl
from jax.experimental.pallas import tpu as pltpu
from jax.sharding import PartitionSpec as P

NEG_FILL = -1e30
BF16, F32 = jnp.bfloat16, jnp.float32
SCALE = math.log2(math.e) / math.sqrt(128)
NT = (((1,), (1,)), ((), ()))
LAST_Z, LAST_HEAD = 10, 5


def split_three(x):
    high = x.astype(BF16).astype(F32)
    rest = x - high
    middle = rest.astype(BF16).astype(F32)
    return [high, middle, rest - middle]


def sample_rows(parts, count):
    lanes = 16 * count
    sample = lax.broadcasted_iota(jnp.int32, (count, lanes), 0)
    mine = sample == lax.broadcasted_iota(jnp.int32, (count, lanes), 1) // 16
    stacked = jnp.concatenate([jnp.where(mine, part, 0.0) for part in parts], 0).astype(BF16)
    place = lax.broadcasted_iota(jnp.int32, (lanes, 128), 0) % 16
    fold = (place == lax.broadcasted_iota(jnp.int32, (lanes, 128), 1) % 16).astype(F32).astype(BF16)
    folded = jnp.dot(stacked, fold, preferred_element_type=F32)
    lane_part = lax.broadcasted_iota(jnp.int32, (count, 128), 1) // 16
    rows = jnp.zeros((count, 128), F32)
    for p in range(len(parts)):
        rows = jnp.where(lane_part == p, folded[p * count : (p + 1) * count], rows)
    return rows


def prefix_kernel(q_ref, kv_ref, near_ref, fk_ref, fv_ref, out_ref):
    key_block, row_block = 256, 256
    depth = kv_ref.shape[0] // 2
    starts = range(0, depth, key_block)
    shards = [
        (kv_ref.at[0:depth], kv_ref.at[depth : 2 * depth]),
        (near_ref.at[0:depth], near_ref.at[depth : 2 * depth]),
        (fk_ref.at[0], fv_ref.at[0]),
        (fk_ref.at[1], fv_ref.at[1]),
    ]
    for at in range(q_ref.shape[0] // row_block):
        q = q_ref[at * row_block : (at + 1) * row_block, :]
        scores = [
            lax.dot_general(q, k[i : i + key_block, :], NT, preferred_element_type=F32) for k, _ in shards for i in starts
        ]
        values = [v[i : i + key_block, :] for _, v in shards for i in starts]
        highest = functools.reduce(jnp.maximum, scores).max(1, keepdims=True)
        totals, weighted = [], []
        for s, v in zip(scores, values):
            p = jnp.exp2((s - highest) * SCALE)
            totals.append(p)
            weighted.append(jnp.dot(p.astype(BF16), v, preferred_element_type=F32))
        total = functools.reduce(jnp.add, totals).sum(1, keepdims=True)
        weighted = functools.reduce(jnp.add, weighted)
        first, count = at * row_block // 16, row_block // 16
        out_ref[first : first + count, 0:8] = weighted.astype(BF16).reshape(count, 8, 2, 128)
        lane = lax.broadcasted_iota(jnp.int32, (row_block, 128), 1)
        stats = jnp.zeros((row_block, 128), F32)
        parts = split_three(highest) + split_three(total)
        for p, part in enumerate(parts):
            stats = jnp.where(lane == p, part, stats)
        stats = stats.T
        rows = sample_rows([stats[p : p + 1] for p in range(len(parts))], count).astype(BF16)
        out_ref[first : first + count, 8] = jnp.broadcast_to(rows[:, None, :], (count, 2, 128))


def suffix_kernel(length_ref, q_ref, sk_ref, sv_ref, nk_ref, nv_ref, o_ref, m_ref, l_ref):
    q = q_ref[...]
    s = lax.dot_general(q, sk_ref[...], NT, preferred_element_type=F32)
    usable = lax.broadcasted_iota(jnp.int32, s.shape, 1) < length_ref[0]
    s = jnp.where(usable, s, NEG_FILL)
    q_wide = q.astype(F32)
    new_keys, new_values = nk_ref[...].astype(F32), nv_ref[...].astype(F32)
    rows = q.shape[0]
    second = lax.broadcasted_iota(jnp.int32, (rows, 1), 0) >= rows // 2
    n0 = (q_wide * new_keys[0:1]).sum(1, keepdims=True)
    n1 = jnp.where(second, (q_wide * new_keys[1:2]).sum(1, keepdims=True), NEG_FILL)
    highest = jnp.maximum(s.max(1, keepdims=True), jnp.maximum(n0, n1))
    p = jnp.where(usable, jnp.exp2((s - highest) * SCALE), 0.0)
    p0 = jnp.exp2((n0 - highest) * SCALE)
    p1 = jnp.where(second, jnp.exp2((n1 - highest) * SCALE), 0.0)
    weighted = jnp.dot(p.astype(BF16), sv_ref[...], preferred_element_type=F32)
    weighted = weighted + p0.astype(BF16).astype(F32) * new_values[0:1] + p1.astype(BF16).astype(F32) * new_values[1:2]
    o_ref[...] = weighted
    m_ref[...] = jnp.broadcast_to(highest, m_ref.shape)
    l_ref[...] = jnp.broadcast_to(p.sum(1, keepdims=True) + p0 + p1, l_ref.shape)


def combine_kernel(got_ref, so_ref, sm_ref, sl_ref, out_ref):
    sources = got_ref.shape[0]
    stats = got_ref[:, 8].astype(F32)[:, 0, :]
    parts = jnp.concatenate([stats, jnp.zeros((128 - sources, 128), F32)], 0).T[:, 0:sources]
    maxima = parts[0:16] + (parts[16:32] + parts[32:48])
    totals = parts[48:64] + (parts[64:80] + parts[80:96])
    own_max, own_total = sm_ref[:, 0:1], sl_ref[:, 0:1]
    top = jnp.maximum(maxima.max(1, keepdims=True), own_max)
    factor = jnp.exp2((maxima - top) * SCALE)
    own_factor = jnp.exp2((own_max - top) * SCALE)
    weight_total = (factor * totals).sum(1, keepdims=True) + own_factor * own_total
    weighted = own_factor * so_ref[...]
    for i in range(sources):
        weighted = weighted + factor[:, i : i + 1] * got_ref[i, 0:8].astype(F32).reshape(16, 128)
    attended = (weighted / weight_total).astype(BF16)
    out_ref[...] = jnp.broadcast_to(attended[None], out_ref.shape)


def project_kernel(place_ref, x_ref, w_ref, far_ref, out_ref):
    samples, rows, hd = x_ref.shape
    group = w_ref.shape[2] // hd
    heads, chunk = out_ref.shape[1:3]
    x = x_ref[...].astype(F32).reshape(samples * rows // group, group, hd)
    x = jnp.swapaxes(x, 0, 1).astype(BF16)
    side = place_ref[0] // 2 * 2
    for ref, at in ((w_ref, side), (far_ref, 2 - side)):
        for core in range(2):
            y = functools.reduce(
                jnp.add,
                [
                    lax.dot_general(
                        x[g], ref[core, :, g * hd : (g + 1) * hd], NT, preferred_element_type=F32
                    )
                    for g in range(group)
                ],
            )
            for block in range(heads):
                shard = (block * samples // heads + LAST_Z) % samples * heads // samples
                out_ref[at + core, (shard - LAST_HEAD) % heads] = y[block * chunk : (block + 1) * chunk]


def finish_kernel(terms_ref, residual_ref, out_ref):
    planes, heads = terms_ref.shape[:2]
    steps = residual_ref.shape[0]
    sums = [functools.reduce(jnp.add, [terms_ref[d, h] for h in range(heads)]) for d in range(planes)]
    for t in range(steps):
        rows = [sums[d][z * steps + t][None] for z in range(sums[0].shape[0] // steps) for d in range(planes)]
        out_ref[t] = (jnp.concatenate(rows, 0) + residual_ref[t].astype(F32)).astype(BF16)


def vmem(n):
    return [pl.BlockSpec(memory_space=pltpu.VMEM)] * n


SMEM = pl.BlockSpec(memory_space=pltpu.SMEM)
PARAMS = pltpu.CompilerParams(vmem_limit_bytes=32 * 1024 * 1024)


def body(
    queries,
    new_keys,
    new_values,
    suffix_keys,
    suffix_values,
    suffix_lengths,
    prefix_keys,
    prefix_values,
    out_weight,
    residual,
):
    steps, _, group, hd = queries.shape
    rows = steps * group
    ctx = lax.axis_size("ctx")
    heads = lax.axis_size("head")
    depth = ctx // 4
    lines = [[4 * ((z + LAST_Z) % depth) + j for z in range(depth)] for j in range(4)]
    halves = [[2 * i + core for i in range(ctx // 2)] for core in range(2)]
    pairs = [[2 * i, 2 * i + 1] for i in range(ctx // 2)]
    planes = [
        [(4 * z + j) * heads + (h + LAST_HEAD) % heads for j in range(4) for h in range(heads)] for z in range(depth)
    ]
    place = lax.axis_index("ctx").astype(jnp.int32)

    def swap(x, bit):
        return lax.ppermute(x, "ctx", [(i, i ^ bit) for i in range(ctx)])

    def exchange(x, groups):
        return lax.all_to_all(x, "ctx", 0, 0, axis_index_groups=groups, tiled=True)

    def both(x):
        return lax.all_gather(x, "ctx", axis=0, axis_index_groups=pairs)

    query_rows = queries.reshape(rows, hd)
    kv = jnp.concatenate([prefix_keys.reshape(-1, hd), prefix_values.reshape(-1, hd)], 0)
    far = swap(kv, 2)
    near = swap(kv, 1)
    copies = jnp.broadcast_to(query_rows[None], (depth, rows, hd))
    line_queries = exchange(copies, lines).reshape(depth * rows, hd)
    half = kv.shape[0] // 2
    far_keys, far_values = both(far[:half]), both(far[half:])

    own = pl.pallas_call(
        suffix_kernel,
        out_shape=[jax.ShapeDtypeStruct((rows, hd), F32)] * 3,
        in_specs=[SMEM] + vmem(5),
        out_specs=vmem(3),
        compiler_params=PARAMS,
        name="suffix_state",
    )(
        suffix_lengths,
        query_rows,
        suffix_keys.reshape(-1, hd),
        suffix_values.reshape(-1, hd),
        new_keys.reshape(-1, hd),
        new_values.reshape(-1, hd),
    )

    partial = pl.pallas_call(
        prefix_kernel,
        out_shape=jax.ShapeDtypeStruct((depth, rows // 2 + 1, 2, hd), BF16),
        in_specs=vmem(5),
        out_specs=vmem(1)[0],
        compiler_params=PARAMS,
        name="prefix_state",
    )(line_queries, kv, near, far_keys, far_values)
    received = exchange(partial, lines)

    weight = out_weight.T
    far_weight = swap(weight, 2)
    weights, far_weights = both(weight), both(far_weight)

    attended = pl.pallas_call(
        combine_kernel,
        out_shape=jax.ShapeDtypeStruct((depth, rows, hd), BF16),
        in_specs=vmem(4),
        out_specs=vmem(1)[0],
        compiler_params=PARAMS,
        name="combine",
    )(received, *own)

    line_rows = exchange(attended, lines)
    columns = weight.shape[0]
    product = pl.pallas_call(
        project_kernel,
        out_shape=jax.ShapeDtypeStruct((4, heads, depth * steps // heads, columns), F32),
        in_specs=[SMEM] + vmem(3),
        out_specs=vmem(1)[0],
        compiler_params=PARAMS,
        name="project",
    )((place % 4).reshape(1), line_rows, weights, far_weights)
    product = product.reshape(4 * heads, depth * steps // heads, columns)
    terms = lax.all_to_all(product, ("ctx", "head"), 0, 0, axis_index_groups=planes, tiled=True)
    return pl.pallas_call(
        finish_kernel,
        out_shape=jax.ShapeDtypeStruct(residual.shape, BF16),
        in_specs=vmem(2),
        out_specs=vmem(1)[0],
        compiler_params=PARAMS,
        name="finish",
    )(terms.reshape(4, heads, depth * steps // heads, columns), residual)


def solution(mesh):
    in_specs = (
        P(None, "ctx", "head", None),
        P(None, "ctx", "head", None),
        P(None, "ctx", "head", None),
        P("ctx", None, "head", None),
        P("ctx", None, "head", None),
        P("ctx"),
        P("ctx", "head", None),
        P("ctx", "head", None),
        P("head", "ctx"),
        P(None, "head", "ctx"),
    )
    out_specs = P(None, "head", "ctx")
    return jax.shard_map(body, mesh=mesh, in_specs=in_specs, out_specs=out_specs, check_vma=False)
```

```python
import functools
import math

import jax
import jax.numpy as jnp
from jax import lax
from jax.experimental import pallas as pl
from jax.experimental.pallas import tpu as pltpu
from jax.sharding import PartitionSpec as P

NEG_FILL = -1e30
BF16, F32 = jnp.bfloat16, jnp.float32
SCALE = math.log2(math.e) / math.sqrt(128)
NT = (((1,), (1,)), ((), ()))
LINE_ORDER = [10, 9, 8, 7, 6, 5, 4, 3, 2, 1, 0, 15, 14, 13, 12, 11]
SIDE_ORDER, HEAD_ORDER = [1, 2, 3, 0], [5, 6, 7, 0, 1, 2, 3, 4]


def split_three(x):
    high = x.astype(BF16).astype(F32)
    rest = x - high
    middle = rest.astype(BF16).astype(F32)
    return [high, middle, rest - middle]


def sample_rows(parts, count):
    lanes = 16 * count
    sample = lax.broadcasted_iota(jnp.int32, (count, lanes), 0)
    mine = sample == lax.broadcasted_iota(jnp.int32, (count, lanes), 1) // 16
    stacked = jnp.concatenate([jnp.where(mine, part, 0.0) for part in parts], 0).astype(BF16)
    place = lax.broadcasted_iota(jnp.int32, (lanes, 128), 0) % 16
    fold = (place == lax.broadcasted_iota(jnp.int32, (lanes, 128), 1) % 16).astype(F32).astype(BF16)
    folded = jnp.dot(stacked, fold, preferred_element_type=F32)
    lane_part = lax.broadcasted_iota(jnp.int32, (count, 128), 1) // 16
    rows = jnp.zeros((count, 128), F32)
    for p in range(len(parts)):
        rows = jnp.where(lane_part == p, folded[p * count : (p + 1) * count], rows)
    return rows


def prefix_kernel(q_ref, kv_ref, near_ref, fk_ref, fv_ref, out_ref):
    key_block, row_block = 256, 128
    depth = kv_ref.shape[0] // 2
    starts = range(0, depth, key_block)
    shards = [
        (kv_ref.at[0:depth], kv_ref.at[depth : 2 * depth]),
        (near_ref.at[0:depth], near_ref.at[depth : 2 * depth]),
        (fk_ref.at[0], fv_ref.at[0]),
        (fk_ref.at[1], fv_ref.at[1]),
    ]
    spans = [slice(at, at + row_block) for at in range(0, q_ref.shape[0], row_block)]
    values = [v[i : i + key_block, :] for _, v in shards for i in starts]
    all_scores = [
        [
            lax.dot_general(q_ref[span, :], k[i : i + key_block, :], NT, preferred_element_type=F32)
            for k, _ in shards
            for i in starts
        ]
        for span in spans
    ]
    for span, scores in zip(spans, all_scores):
        highest = functools.reduce(jnp.maximum, scores).max(1, keepdims=True)
        totals, weighted = [], []
        for s, v in zip(scores, values):
            p = jnp.exp2((s - highest) * SCALE)
            totals.append(p)
            weighted.append(jnp.dot(p.astype(BF16), v, preferred_element_type=F32))
        total = functools.reduce(jnp.add, totals).sum(1, keepdims=True)
        weighted = functools.reduce(jnp.add, weighted)
        first, count = span.start // 16, row_block // 16
        out_ref[first : first + count, 0:8] = weighted.astype(BF16).reshape(count, 8, 2, 128)
        lane = lax.broadcasted_iota(jnp.int32, (row_block, 128), 1)
        stats = jnp.zeros((row_block, 128), F32)
        parts = split_three(highest) + split_three(total)
        for p, part in enumerate(parts):
            stats = jnp.where(lane == p, part, stats)
        stats = stats.T
        rows = sample_rows([stats[p : p + 1] for p in range(len(parts))], count).astype(BF16)
        out_ref[first : first + count, 8] = jnp.broadcast_to(rows[:, None, :], (count, 2, 128))


def suffix_kernel(length_ref, q_ref, sk_ref, sv_ref, nk_ref, nv_ref, o_ref, m_ref, l_ref):
    q = q_ref[...]
    s = lax.dot_general(q, sk_ref[...], NT, preferred_element_type=F32)
    usable = lax.broadcasted_iota(jnp.int32, s.shape, 1) < length_ref[0]
    s = jnp.where(usable, s, NEG_FILL)
    q_wide = q.astype(F32)
    new_keys, new_values = nk_ref[...].astype(F32), nv_ref[...].astype(F32)
    rows = q.shape[0]
    second = lax.broadcasted_iota(jnp.int32, (rows, 1), 0) >= rows // 2
    n0 = (q_wide * new_keys[0:1]).sum(1, keepdims=True)
    n1 = jnp.where(second, (q_wide * new_keys[1:2]).sum(1, keepdims=True), NEG_FILL)
    highest = jnp.maximum(s.max(1, keepdims=True), jnp.maximum(n0, n1))
    p = jnp.where(usable, jnp.exp2((s - highest) * SCALE), 0.0)
    p0 = jnp.exp2((n0 - highest) * SCALE)
    p1 = jnp.where(second, jnp.exp2((n1 - highest) * SCALE), 0.0)
    weighted = jnp.dot(p.astype(BF16), sv_ref[...], preferred_element_type=F32)
    weighted = weighted + p0.astype(BF16).astype(F32) * new_values[0:1] + p1.astype(BF16).astype(F32) * new_values[1:2]
    o_ref[...] = weighted
    m_ref[...] = jnp.broadcast_to(highest, m_ref.shape)
    l_ref[...] = jnp.broadcast_to(p.sum(1, keepdims=True) + p0 + p1, l_ref.shape)


def combine_kernel(got_ref, so_ref, sm_ref, sl_ref, out_ref):
    sources = got_ref.shape[0]
    stats = got_ref[:, 8].astype(F32)[:, 0, :]
    parts = jnp.concatenate([stats, jnp.zeros((128 - sources, 128), F32)], 0).T[:, 0:sources]
    maxima = parts[0:16] + (parts[16:32] + parts[32:48])
    totals = parts[48:64] + (parts[64:80] + parts[80:96])
    own_max, own_total = sm_ref[:, 0:1], sl_ref[:, 0:1]
    top = jnp.maximum(maxima.max(1, keepdims=True), own_max)
    factor = jnp.exp2((maxima - top) * SCALE)
    own_factor = jnp.exp2((own_max - top) * SCALE)
    weight_total = (factor * totals).sum(1, keepdims=True) + own_factor * own_total
    weighted = own_factor * so_ref[...]
    for i in range(sources):
        weighted = weighted + factor[:, i : i + 1] * got_ref[i, 0:8].astype(F32).reshape(16, 128)
    attended = (weighted / weight_total).astype(BF16)
    out_ref[...] = jnp.broadcast_to(attended[None], out_ref.shape)


def project_kernel(place_ref, x_ref, w_ref, far_ref, out_ref):
    samples, rows, hd = x_ref.shape
    group = w_ref.shape[2] // hd
    heads, chunk = out_ref.shape[1:3]
    steps = rows // group
    x = x_ref[...].astype(F32).reshape(samples * steps, group, hd)
    x = jnp.swapaxes(x, 0, 1).astype(BF16)
    side = place_ref[0] // 2 * 2
    for ref, at in ((w_ref, side), (far_ref, 2 - side)):
        for core in range(2):
            y = functools.reduce(
                jnp.add,
                [
                    lax.dot_general(
                        x[g], ref[core, :, g * hd : (g + 1) * hd], NT, preferred_element_type=F32
                    )
                    for g in range(group)
                ],
            )
            to = functools.reduce(jnp.add, [jnp.where(at + core == d, p, 0) for p, d in enumerate(SIDE_ORDER)])
            for member, z in enumerate(LINE_ORDER):
                shard, slot = divmod(z * heads, samples)
                first = slot * chunk // samples
                out_ref[to, HEAD_ORDER.index(shard), first : first + steps] = y[member * steps : (member + 1) * steps]


def finish_kernel(terms_ref, residual_ref, out_ref):
    planes, heads = terms_ref.shape[:2]
    steps = residual_ref.shape[0]
    sums = [
        functools.reduce(jnp.add, [terms_ref[SIDE_ORDER.index(d), h] for h in range(heads)]) for d in range(planes)
    ]
    for t in range(steps):
        rows = [sums[d][z * steps + t][None] for z in range(sums[0].shape[0] // steps) for d in range(planes)]
        out_ref[t] = (jnp.concatenate(rows, 0) + residual_ref[t].astype(F32)).astype(BF16)


def vmem(n):
    return [pl.BlockSpec(memory_space=pltpu.VMEM)] * n


SMEM = pl.BlockSpec(memory_space=pltpu.SMEM)
PARAMS = pltpu.CompilerParams(vmem_limit_bytes=32 * 1024 * 1024)


def body(
    queries,
    new_keys,
    new_values,
    suffix_keys,
    suffix_values,
    suffix_lengths,
    prefix_keys,
    prefix_values,
    out_weight,
    residual,
):
    steps, _, group, hd = queries.shape
    rows = steps * group
    ctx = lax.axis_size("ctx")
    heads = lax.axis_size("head")
    depth = ctx // 4
    lines = [[4 * z + j for z in LINE_ORDER] for j in range(4)]
    halves = [[2 * i + core for i in range(ctx // 2)] for core in range(2)]
    pairs = [[2 * i, 2 * i + 1] for i in range(ctx // 2)]
    planes = [[(4 * z + j) * heads + h for j in SIDE_ORDER for h in HEAD_ORDER] for z in range(depth)]
    place = lax.axis_index("ctx").astype(jnp.int32)

    def swap(x, bit):
        return lax.ppermute(x, "ctx", [(i, i ^ bit) for i in range(ctx)])

    def exchange(x, groups):
        return lax.all_to_all(x, "ctx", 0, 0, axis_index_groups=groups, tiled=True)

    def both(x):
        return lax.all_gather(x, "ctx", axis=0, axis_index_groups=pairs)

    query_rows = queries.reshape(rows, hd)
    kv = jnp.concatenate([prefix_keys.reshape(-1, hd), prefix_values.reshape(-1, hd)], 0)
    far = swap(kv, 2)
    near = swap(kv, 1)
    copies = jnp.broadcast_to(query_rows[None], (depth, rows, hd))
    line_queries = exchange(copies, lines).reshape(depth * rows, hd)
    half = kv.shape[0] // 2
    far_keys, far_values = both(far[:half]), both(far[half:])

    own = pl.pallas_call(
        suffix_kernel,
        out_shape=[jax.ShapeDtypeStruct((rows, hd), F32)] * 3,
        in_specs=[SMEM] + vmem(5),
        out_specs=vmem(3),
        compiler_params=PARAMS,
        name="suffix_state",
    )(
        suffix_lengths,
        query_rows,
        suffix_keys.reshape(-1, hd),
        suffix_values.reshape(-1, hd),
        new_keys.reshape(-1, hd),
        new_values.reshape(-1, hd),
    )

    partial = pl.pallas_call(
        prefix_kernel,
        out_shape=jax.ShapeDtypeStruct((depth, rows // 2 + 1, 2, hd), BF16),
        in_specs=vmem(5),
        out_specs=vmem(1)[0],
        compiler_params=PARAMS,
        name="prefix_state",
    )(line_queries, kv, near, far_keys, far_values)
    received = exchange(partial, lines)

    weight = out_weight.T
    far_weight = swap(weight, 2)
    weights, far_weights = both(weight), both(far_weight)

    attended = pl.pallas_call(
        combine_kernel,
        out_shape=jax.ShapeDtypeStruct((depth, rows, hd), BF16),
        in_specs=vmem(4),
        out_specs=vmem(1)[0],
        compiler_params=PARAMS,
        name="combine",
    )(received, *own)

    line_rows = exchange(attended, lines)
    columns = weight.shape[0]
    product = pl.pallas_call(
        project_kernel,
        out_shape=jax.ShapeDtypeStruct((4, heads, depth * steps // heads, columns), F32),
        in_specs=[SMEM] + vmem(3),
        out_specs=vmem(1)[0],
        compiler_params=PARAMS,
        name="project",
    )((place % 4).reshape(1), line_rows, weights, far_weights)
    product = product.reshape(4 * heads, depth * steps // heads, columns)
    terms = lax.all_to_all(product, ("ctx", "head"), 0, 0, axis_index_groups=planes, tiled=True)
    return pl.pallas_call(
        finish_kernel,
        out_shape=jax.ShapeDtypeStruct(residual.shape, BF16),
        in_specs=vmem(2),
        out_specs=vmem(1)[0],
        compiler_params=PARAMS,
        name="finish",
    )(terms.reshape(4, heads, depth * steps // heads, columns), residual)


def solution(mesh):
    in_specs = (
        P(None, "ctx", "head", None),
        P(None, "ctx", "head", None),
        P(None, "ctx", "head", None),
        P("ctx", None, "head", None),
        P("ctx", None, "head", None),
        P("ctx"),
        P("ctx", "head", None),
        P("ctx", "head", None),
        P("head", "ctx"),
        P(None, "head", "ctx"),
    )
    out_specs = P(None, "head", "ctx")
    return jax.shard_map(body, mesh=mesh, in_specs=in_specs, out_specs=out_specs, check_vma=False)
```

```python
import functools
import math

import jax
import jax.numpy as jnp
from jax import lax
from jax.experimental import pallas as pl
from jax.experimental.pallas import tpu as pltpu
from jax.sharding import PartitionSpec as P

NEG_FILL = -1e30
BF16, F32 = jnp.bfloat16, jnp.float32
SCALE = math.log2(math.e) / math.sqrt(128)
NT = (((1,), (1,)), ((), ()))
LINE_ORDER = [11, 10, 12, 9, 13, 8, 14, 7, 15, 6, 0, 5, 1, 4, 2, 3]
SIDE_ORDER, HEAD_ORDER = [1, 2, 3, 0], [5, 6, 7, 0, 1, 2, 3, 4]


def split_three(x):
    high = x.astype(BF16).astype(F32)
    rest = x - high
    middle = rest.astype(BF16).astype(F32)
    return [high, middle, rest - middle]


def sample_rows(parts, count):
    lanes = 16 * count
    sample = lax.broadcasted_iota(jnp.int32, (count, lanes), 0)
    mine = sample == lax.broadcasted_iota(jnp.int32, (count, lanes), 1) // 16
    stacked = jnp.concatenate([jnp.where(mine, part, 0.0) for part in parts], 0).astype(BF16)
    place = lax.broadcasted_iota(jnp.int32, (lanes, 128), 0) % 16
    fold = (place == lax.broadcasted_iota(jnp.int32, (lanes, 128), 1) % 16).astype(F32).astype(BF16)
    folded = jnp.dot(stacked, fold, preferred_element_type=F32)
    lane_part = lax.broadcasted_iota(jnp.int32, (count, 128), 1) // 16
    rows = jnp.zeros((count, 128), F32)
    for p in range(len(parts)):
        rows = jnp.where(lane_part == p, folded[p * count : (p + 1) * count], rows)
    return rows


def prefix_kernel(q_ref, kv_ref, near_ref, fk_ref, fv_ref, out_ref):
    key_block, row_block = 256, 128
    depth = kv_ref.shape[0] // 2
    starts = range(0, depth, key_block)
    shards = [
        (kv_ref.at[0:depth], kv_ref.at[depth : 2 * depth]),
        (near_ref.at[0:depth], near_ref.at[depth : 2 * depth]),
        (fk_ref.at[0], fv_ref.at[0]),
        (fk_ref.at[1], fv_ref.at[1]),
    ]
    spans = [slice(at, at + row_block) for at in range(0, q_ref.shape[0], row_block)]
    values = [v[i : i + key_block, :] for _, v in shards for i in starts]
    all_scores = [
        [
            lax.dot_general(q_ref[span, :], k[i : i + key_block, :], NT, preferred_element_type=F32)
            for k, _ in shards
            for i in starts
        ]
        for span in spans
    ]
    for span, scores in zip(spans, all_scores):
        highest = functools.reduce(jnp.maximum, scores).max(1, keepdims=True)
        totals, weighted = [], []
        for s, v in zip(scores, values):
            p = jnp.exp2((s - highest) * SCALE)
            totals.append(p)
            weighted.append(jnp.dot(p.astype(BF16), v, preferred_element_type=F32))
        total = functools.reduce(jnp.add, totals).sum(1, keepdims=True)
        weighted = functools.reduce(jnp.add, weighted)
        first, count = span.start // 16, row_block // 16
        out_ref[first : first + count, 0:8] = weighted.astype(BF16).reshape(count, 8, 2, 128)
        lane = lax.broadcasted_iota(jnp.int32, (row_block, 128), 1)
        stats = jnp.zeros((row_block, 128), F32)
        parts = split_three(highest) + split_three(total)
        for p, part in enumerate(parts):
            stats = jnp.where(lane == p, part, stats)
        stats = stats.T
        rows = sample_rows([stats[p : p + 1] for p in range(len(parts))], count).astype(BF16)
        out_ref[first : first + count, 8] = jnp.broadcast_to(rows[:, None, :], (count, 2, 128))


def suffix_kernel(length_ref, q_ref, sk_ref, sv_ref, nk_ref, nv_ref, o_ref, m_ref, l_ref):
    q = q_ref[...]
    s = lax.dot_general(q, sk_ref[...], NT, preferred_element_type=F32)
    usable = lax.broadcasted_iota(jnp.int32, s.shape, 1) < length_ref[0]
    s = jnp.where(usable, s, NEG_FILL)
    q_wide = q.astype(F32)
    new_keys, new_values = nk_ref[...].astype(F32), nv_ref[...].astype(F32)
    rows = q.shape[0]
    second = lax.broadcasted_iota(jnp.int32, (rows, 1), 0) >= rows // 2
    n0 = (q_wide * new_keys[0:1]).sum(1, keepdims=True)
    n1 = jnp.where(second, (q_wide * new_keys[1:2]).sum(1, keepdims=True), NEG_FILL)
    highest = jnp.maximum(s.max(1, keepdims=True), jnp.maximum(n0, n1))
    p = jnp.where(usable, jnp.exp2((s - highest) * SCALE), 0.0)
    p0 = jnp.exp2((n0 - highest) * SCALE)
    p1 = jnp.where(second, jnp.exp2((n1 - highest) * SCALE), 0.0)
    weighted = jnp.dot(p.astype(BF16), sv_ref[...], preferred_element_type=F32)
    weighted = weighted + p0.astype(BF16).astype(F32) * new_values[0:1] + p1.astype(BF16).astype(F32) * new_values[1:2]
    o_ref[...] = weighted
    m_ref[...] = jnp.broadcast_to(highest, m_ref.shape)
    l_ref[...] = jnp.broadcast_to(p.sum(1, keepdims=True) + p0 + p1, l_ref.shape)


def combine_kernel(got_ref, so_ref, sm_ref, sl_ref, out_ref):
    sources = got_ref.shape[0]
    stats = got_ref[:, 8].astype(F32)[:, 0, :]
    parts = jnp.concatenate([stats, jnp.zeros((128 - sources, 128), F32)], 0).T[:, 0:sources]
    maxima = parts[0:16] + (parts[16:32] + parts[32:48])
    totals = parts[48:64] + (parts[64:80] + parts[80:96])
    own_max, own_total = sm_ref[:, 0:1], sl_ref[:, 0:1]
    top = jnp.maximum(maxima.max(1, keepdims=True), own_max)
    factor = jnp.exp2((maxima - top) * SCALE)
    own_factor = jnp.exp2((own_max - top) * SCALE)
    weight_total = (factor * totals).sum(1, keepdims=True) + own_factor * own_total
    weighted = own_factor * so_ref[...]
    for i in range(sources):
        weighted = weighted + factor[:, i : i + 1] * got_ref[i, 0:8].astype(F32).reshape(16, 128)
    attended = (weighted / weight_total).astype(BF16)
    out_ref[...] = jnp.broadcast_to(attended[None], out_ref.shape)


def project_kernel(place_ref, x_ref, w_ref, far_ref, out_ref):
    samples, rows, hd = x_ref.shape
    group = w_ref.shape[2] // hd
    heads, chunk = out_ref.shape[1:3]
    steps = rows // group
    x = x_ref[...].astype(F32).reshape(samples * steps, group, hd)
    x = jnp.swapaxes(x, 0, 1).astype(BF16)
    side = place_ref[0] // 2 * 2
    for ref, at in ((w_ref, side), (far_ref, 2 - side)):
        for core in range(2):
            y = functools.reduce(
                jnp.add,
                [
                    lax.dot_general(
                        x[g], ref[core, :, g * hd : (g + 1) * hd], NT, preferred_element_type=F32
                    )
                    for g in range(group)
                ],
            )
            to = functools.reduce(jnp.add, [jnp.where(at + core == d, p, 0) for p, d in enumerate(SIDE_ORDER)])
            for member, z in enumerate(LINE_ORDER):
                shard, slot = divmod(z * heads, samples)
                first = slot * chunk // samples
                out_ref[to, HEAD_ORDER.index(shard), first : first + steps] = y[member * steps : (member + 1) * steps].astype(BF16)


def finish_kernel(terms_ref, residual_ref, out_ref):
    planes, heads = terms_ref.shape[:2]
    steps = residual_ref.shape[0]
    sums = [
        functools.reduce(jnp.add, [terms_ref[SIDE_ORDER.index(d), h].astype(F32) for h in range(heads)]) for d in range(planes)
    ]
    for t in range(steps):
        rows = [sums[d][z * steps + t][None] for z in range(sums[0].shape[0] // steps) for d in range(planes)]
        out_ref[t] = (jnp.concatenate(rows, 0) + residual_ref[t].astype(F32)).astype(BF16)


def vmem(n):
    return [pl.BlockSpec(memory_space=pltpu.VMEM)] * n


SMEM = pl.BlockSpec(memory_space=pltpu.SMEM)
PARAMS = pltpu.CompilerParams(vmem_limit_bytes=32 * 1024 * 1024)


def body(
    queries,
    new_keys,
    new_values,
    suffix_keys,
    suffix_values,
    suffix_lengths,
    prefix_keys,
    prefix_values,
    out_weight,
    residual,
):
    steps, _, group, hd = queries.shape
    rows = steps * group
    ctx = lax.axis_size("ctx")
    heads = lax.axis_size("head")
    depth = ctx // 4
    lines = [[4 * z + j for z in LINE_ORDER] for j in range(4)]
    halves = [[2 * i + core for i in range(ctx // 2)] for core in range(2)]
    pairs = [[2 * i, 2 * i + 1] for i in range(ctx // 2)]
    planes = [[(4 * z + j) * heads + h for j in SIDE_ORDER for h in HEAD_ORDER] for z in range(depth)]
    place = lax.axis_index("ctx").astype(jnp.int32)

    def swap(x, bit):
        return lax.ppermute(x, "ctx", [(i, i ^ bit) for i in range(ctx)])

    def exchange(x, groups):
        return lax.all_to_all(x, "ctx", 0, 0, axis_index_groups=groups, tiled=True)

    def both(x):
        return lax.all_gather(x, "ctx", axis=0, axis_index_groups=pairs)

    query_rows = queries.reshape(rows, hd)
    kv = jnp.concatenate([prefix_keys.reshape(-1, hd), prefix_values.reshape(-1, hd)], 0)
    far = swap(kv, 2)
    near = swap(kv, 1)
    copies = jnp.broadcast_to(query_rows[None], (depth, rows, hd))
    line_queries = exchange(copies, lines).reshape(depth * rows, hd)
    half = kv.shape[0] // 2
    far_keys, far_values = both(far[:half]), both(far[half:])

    own = pl.pallas_call(
        suffix_kernel,
        out_shape=[jax.ShapeDtypeStruct((rows, hd), F32)] * 3,
        in_specs=[SMEM] + vmem(5),
        out_specs=vmem(3),
        compiler_params=PARAMS,
        name="suffix_state",
    )(
        suffix_lengths,
        query_rows,
        suffix_keys.reshape(-1, hd),
        suffix_values.reshape(-1, hd),
        new_keys.reshape(-1, hd),
        new_values.reshape(-1, hd),
    )

    partial = pl.pallas_call(
        prefix_kernel,
        out_shape=jax.ShapeDtypeStruct((depth, rows // 2 + 1, 2, hd), BF16),
        in_specs=vmem(5),
        out_specs=vmem(1)[0],
        compiler_params=PARAMS,
        name="prefix_state",
    )(line_queries, kv, near, far_keys, far_values)
    received = exchange(partial, lines)

    weight = out_weight.T
    far_weight = swap(weight, 2)
    weights, far_weights = both(weight), both(far_weight)

    attended = pl.pallas_call(
        combine_kernel,
        out_shape=jax.ShapeDtypeStruct((depth, rows, hd), BF16),
        in_specs=vmem(4),
        out_specs=vmem(1)[0],
        compiler_params=PARAMS,
        name="combine",
    )(received, *own)

    line_rows = exchange(attended, lines)
    columns = weight.shape[0]
    product = pl.pallas_call(
        project_kernel,
        out_shape=jax.ShapeDtypeStruct((4, heads, depth * steps // heads, columns), BF16),
        in_specs=[SMEM] + vmem(3),
        out_specs=vmem(1)[0],
        compiler_params=PARAMS,
        name="project",
    )((place % 4).reshape(1), line_rows, weights, far_weights)
    product = product.reshape(4 * heads, depth * steps // heads, columns)
    terms = lax.all_to_all(product, ("ctx", "head"), 0, 0, axis_index_groups=planes, tiled=True)
    return pl.pallas_call(
        finish_kernel,
        out_shape=jax.ShapeDtypeStruct(residual.shape, BF16),
        in_specs=vmem(2),
        out_specs=vmem(1)[0],
        compiler_params=PARAMS,
        name="finish",
    )(terms.reshape(4, heads, depth * steps // heads, columns), residual)


def solution(mesh):
    in_specs = (
        P(None, "ctx", "head", None),
        P(None, "ctx", "head", None),
        P(None, "ctx", "head", None),
        P("ctx", None, "head", None),
        P("ctx", None, "head", None),
        P("ctx"),
        P("ctx", "head", None),
        P("ctx", "head", None),
        P("head", "ctx"),
        P(None, "head", "ctx"),
    )
    out_specs = P(None, "head", "ctx")
    return jax.shard_map(body, mesh=mesh, in_specs=in_specs, out_specs=out_specs, check_vma=False)
```

```python
import functools
import math

import jax
import jax.numpy as jnp
from jax import lax
from jax.experimental import pallas as pl
from jax.experimental.pallas import tpu as pltpu
from jax.sharding import PartitionSpec as P

NEG_FILL = -1e30
BF16, F32 = jnp.bfloat16, jnp.float32
SCALE = math.log2(math.e) / math.sqrt(128)
NT = (((1,), (1,)), ((), ()))
EARLY_Z = 5
LINE_ORDER = [10, 9, 8, 7, 6, 5, 4, 3, 2, 1, 0, 15, 14, 13, 12, 11]
SIDE_ORDER, HEAD_ORDER = [1, 2, 3, 0], [5, 6, 7, 0, 1, 2, 3, 4]


def split_three(x):
    high = x.astype(BF16).astype(F32)
    rest = x - high
    middle = rest.astype(BF16).astype(F32)
    return [high, middle, rest - middle]


def sample_rows(parts, count):
    lanes = 16 * count
    sample = lax.broadcasted_iota(jnp.int32, (count, lanes), 0)
    mine = sample == lax.broadcasted_iota(jnp.int32, (count, lanes), 1) // 16
    stacked = jnp.concatenate([jnp.where(mine, part, 0.0) for part in parts], 0).astype(BF16)
    place = lax.broadcasted_iota(jnp.int32, (lanes, 128), 0) % 16
    fold = (place == lax.broadcasted_iota(jnp.int32, (lanes, 128), 1) % 16).astype(F32).astype(BF16)
    folded = jnp.dot(stacked, fold, preferred_element_type=F32)
    lane_part = lax.broadcasted_iota(jnp.int32, (count, 128), 1) // 16
    rows = jnp.zeros((count, 128), F32)
    for p in range(len(parts)):
        rows = jnp.where(lane_part == p, folded[p * count : (p + 1) * count], rows)
    return rows


def hand_on_kernel(_, out_ref):
    out_ref[...] = jnp.zeros_like(out_ref)


def untouched_kernel(_, out_ref):
    pass


def prefix_kernel(
    early_ref, q_ref, kv_ref, early_near_ref, late_near_ref, fk_ref, fv_ref, out_ref, near_ref, sems
):
    depth = kv_ref.shape[0] // 2
    k_ref, v_ref = kv_ref.at[0:depth], kv_ref.at[depth : 2 * depth]

    def moves(source):
        return [
            pltpu.make_async_copy(source.at[part], near_ref.at[part], sems.at[i])
            for i, part in enumerate((pl.ds(0, depth), pl.ds(depth, depth)))
        ]

    @pl.when(early_ref[0] > 0)
    def _():
        for move in moves(early_near_ref):
            move.start()

    @pl.when(early_ref[0] <= 0)
    def _():
        for move in moves(late_near_ref):
            move.start()

    def arrived():
        @pl.when(early_ref[0] > 0)
        def _():
            for move in moves(early_near_ref):
                move.wait()

        @pl.when(early_ref[0] <= 0)
        def _():
            for move in moves(late_near_ref):
                move.wait()

    prefix_state(q_ref, k_ref, v_ref, near_ref, fk_ref, fv_ref, out_ref, arrived)


def prefix_state(q_ref, k_ref, v_ref, near_ref, fk_ref, fv_ref, out_ref, arrived):
    key_block, row_block = 256, 128
    depth = k_ref.shape[0]
    starts = range(0, depth, key_block)
    shards = [
        (k_ref, v_ref),
        (fk_ref.at[0], fv_ref.at[0]),
        (fk_ref.at[1], fv_ref.at[1]),
        (near_ref.at[0:depth], near_ref.at[depth : 2 * depth]),
    ]
    spans = [slice(at, at + row_block) for at in range(0, q_ref.shape[0], row_block)]
    def score(span, k):
        return [
            lax.dot_general(q_ref[span, :], k[i : i + key_block, :], NT, preferred_element_type=F32) for i in starts
        ]

    held = [[s for k, _ in shards[:-1] for s in score(span, k)] for span in spans]
    arrived()
    all_scores = [scores + score(span, shards[-1][0]) for span, scores in zip(spans, held)]
    values = [v[i : i + key_block, :] for _, v in shards for i in starts]
    for span, scores in zip(spans, all_scores):
        highest = functools.reduce(jnp.maximum, scores).max(1, keepdims=True)
        totals, weighted = [], []
        for s, v in zip(scores, values):
            p = jnp.exp2((s - highest) * SCALE)
            totals.append(p)
            weighted.append(jnp.dot(p.astype(BF16), v, preferred_element_type=F32))
        total = functools.reduce(jnp.add, totals).sum(1, keepdims=True)
        weighted = functools.reduce(jnp.add, weighted)
        first, count = span.start // 16, row_block // 16
        out_ref[first : first + count, 0:8] = weighted.astype(BF16).reshape(count, 8, 2, 128)
        lane = lax.broadcasted_iota(jnp.int32, (row_block, 128), 1)
        stats = jnp.zeros((row_block, 128), F32)
        parts = split_three(highest) + split_three(total)
        for p, part in enumerate(parts):
            stats = jnp.where(lane == p, part, stats)
        stats = stats.T
        rows = sample_rows([stats[p : p + 1] for p in range(len(parts))], count).astype(BF16)
        out_ref[first : first + count, 8] = jnp.broadcast_to(rows[:, None, :], (count, 2, 128))


def suffix_kernel(length_ref, q_ref, sk_ref, sv_ref, nk_ref, nv_ref, o_ref, m_ref, l_ref):
    q = q_ref[...]
    s = lax.dot_general(q, sk_ref[...], NT, preferred_element_type=F32)
    usable = lax.broadcasted_iota(jnp.int32, s.shape, 1) < length_ref[0]
    s = jnp.where(usable, s, NEG_FILL)
    q_wide = q.astype(F32)
    new_keys, new_values = nk_ref[...].astype(F32), nv_ref[...].astype(F32)
    rows = q.shape[0]
    second = lax.broadcasted_iota(jnp.int32, (rows, 1), 0) >= rows // 2
    n0 = (q_wide * new_keys[0:1]).sum(1, keepdims=True)
    n1 = jnp.where(second, (q_wide * new_keys[1:2]).sum(1, keepdims=True), NEG_FILL)
    highest = jnp.maximum(s.max(1, keepdims=True), jnp.maximum(n0, n1))
    p = jnp.where(usable, jnp.exp2((s - highest) * SCALE), 0.0)
    p0 = jnp.exp2((n0 - highest) * SCALE)
    p1 = jnp.where(second, jnp.exp2((n1 - highest) * SCALE), 0.0)
    weighted = jnp.dot(p.astype(BF16), sv_ref[...], preferred_element_type=F32)
    weighted = weighted + p0.astype(BF16).astype(F32) * new_values[0:1] + p1.astype(BF16).astype(F32) * new_values[1:2]
    o_ref[...] = weighted
    m_ref[...] = jnp.broadcast_to(highest, m_ref.shape)
    l_ref[...] = jnp.broadcast_to(p.sum(1, keepdims=True) + p0 + p1, l_ref.shape)


def combine_kernel(got_ref, so_ref, sm_ref, sl_ref, out_ref):
    sources = got_ref.shape[0]
    stats = got_ref[:, 8].astype(F32)[:, 0, :]
    parts = jnp.concatenate([stats, jnp.zeros((128 - sources, 128), F32)], 0).T[:, 0:sources]
    maxima = parts[0:16] + (parts[16:32] + parts[32:48])
    totals = parts[48:64] + (parts[64:80] + parts[80:96])
    own_max, own_total = sm_ref[:, 0:1], sl_ref[:, 0:1]
    top = jnp.maximum(maxima.max(1, keepdims=True), own_max)
    factor = jnp.exp2((maxima - top) * SCALE)
    own_factor = jnp.exp2((own_max - top) * SCALE)
    weight_total = (factor * totals).sum(1, keepdims=True) + own_factor * own_total
    weighted = own_factor * so_ref[...]
    for i in range(sources):
        weighted = weighted + factor[:, i : i + 1] * got_ref[i, 0:8].astype(F32).reshape(16, 128)
    attended = (weighted / weight_total).astype(BF16)
    out_ref[...] = jnp.broadcast_to(attended[None], out_ref.shape)


def project_kernel(place_ref, x_ref, w_ref, far_ref, out_ref):
    samples, rows, hd = x_ref.shape
    group = w_ref.shape[2] // hd
    heads, chunk = out_ref.shape[1:3]
    steps = rows // group
    x = x_ref[...].astype(F32).reshape(samples * steps, group, hd)
    x = jnp.swapaxes(x, 0, 1).astype(BF16)
    side = place_ref[0] // 2 * 2
    for ref, at in ((w_ref, side), (far_ref, 2 - side)):
        for core in range(2):
            y = functools.reduce(
                jnp.add,
                [
                    lax.dot_general(
                        x[g], ref[core, :, g * hd : (g + 1) * hd], NT, preferred_element_type=F32
                    )
                    for g in range(group)
                ],
            )
            to = functools.reduce(jnp.add, [jnp.where(at + core == d, p, 0) for p, d in enumerate(SIDE_ORDER)])
            for member, z in enumerate(LINE_ORDER):
                shard, slot = divmod(z * heads, samples)
                first = slot * chunk // samples
                out_ref[to, HEAD_ORDER.index(shard), first : first + steps] = y[member * steps : (member + 1) * steps]


def finish_kernel(terms_ref, residual_ref, out_ref):
    planes, heads = terms_ref.shape[:2]
    steps = residual_ref.shape[0]
    sums = [
        functools.reduce(jnp.add, [terms_ref[SIDE_ORDER.index(d), h] for h in range(heads)]) for d in range(planes)
    ]
    for t in range(steps):
        rows = [sums[d][z * steps + t][None] for z in range(sums[0].shape[0] // steps) for d in range(planes)]
        out_ref[t] = (jnp.concatenate(rows, 0) + residual_ref[t].astype(F32)).astype(BF16)


def vmem(n):
    return [pl.BlockSpec(memory_space=pltpu.VMEM)] * n


SMEM = pl.BlockSpec(memory_space=pltpu.SMEM)
PARAMS = pltpu.CompilerParams(vmem_limit_bytes=32 * 1024 * 1024)


def body(
    queries,
    new_keys,
    new_values,
    suffix_keys,
    suffix_values,
    suffix_lengths,
    prefix_keys,
    prefix_values,
    out_weight,
    residual,
):
    steps, _, group, hd = queries.shape
    rows = steps * group
    ctx = lax.axis_size("ctx")
    heads = lax.axis_size("head")
    depth = ctx // 4
    lines = [[4 * z + j for z in LINE_ORDER] for j in range(4)]
    halves = [[2 * i + core for i in range(ctx // 2)] for core in range(2)]
    pairs = [[2 * i, 2 * i + 1] for i in range(ctx // 2)]
    planes = [[(4 * z + j) * heads + h for j in SIDE_ORDER for h in HEAD_ORDER] for z in range(depth)]
    place = lax.axis_index("ctx").astype(jnp.int32)

    def swap(x, bit):
        return lax.ppermute(x, "ctx", [(i, i ^ bit) for i in range(ctx)])

    def early_swap(x):
        near = swap(x, 1)
        after = pl.pallas_call(
            hand_on_kernel,
            out_shape=jax.ShapeDtypeStruct((rows, hd), BF16),
            in_specs=[pl.BlockSpec(memory_space=pl.ANY)],
            out_specs=vmem(1)[0],
            compiler_params=PARAMS,
            name="hand_on",
        )(near)
        return near, after

    def untouched(x):
        return pl.pallas_call(
            untouched_kernel,
            out_shape=jax.ShapeDtypeStruct(x.shape, x.dtype),
            in_specs=[pl.BlockSpec(memory_space=pl.ANY)],
            out_specs=pl.BlockSpec(memory_space=pl.ANY),
            compiler_params=PARAMS,
            name="untouched",
        )(x)

    def exchange(x, groups):
        return lax.all_to_all(x, "ctx", 0, 0, axis_index_groups=groups, tiled=True)

    def both(x):
        return lax.all_gather(x, "ctx", axis=0, axis_index_groups=pairs)

    query_rows = queries.reshape(rows, hd)
    kv = jnp.concatenate([prefix_keys.reshape(-1, hd), prefix_values.reshape(-1, hd)], 0)
    far = swap(kv, 2)
    early = place // 4 < EARLY_Z
    early_near, nothing = lax.cond(early, early_swap, lambda x: (untouched(x), jnp.zeros((rows, hd), BF16)), kv)
    copies = jnp.broadcast_to((query_rows + nothing)[None], (depth, rows, hd))
    line_queries = exchange(copies, lines).reshape(depth * rows, hd)
    late_near = lax.cond(early, lambda x: untouched(x), lambda x: swap(x, 1), kv)
    half = kv.shape[0] // 2
    far_keys, far_values = both(far[:half]), both(far[half:])

    own = pl.pallas_call(
        suffix_kernel,
        out_shape=[jax.ShapeDtypeStruct((rows, hd), F32)] * 3,
        in_specs=[SMEM] + vmem(5),
        out_specs=vmem(3),
        compiler_params=PARAMS,
        name="suffix_state",
    )(
        suffix_lengths,
        query_rows,
        suffix_keys.reshape(-1, hd),
        suffix_values.reshape(-1, hd),
        new_keys.reshape(-1, hd),
        new_values.reshape(-1, hd),
    )

    partial = pl.pallas_call(
        prefix_kernel,
        out_shape=jax.ShapeDtypeStruct((depth, rows // 2 + 1, 2, hd), BF16),
        in_specs=[SMEM] + vmem(2) + [pl.BlockSpec(memory_space=pl.ANY)] * 2 + vmem(2),
        out_specs=vmem(1)[0],
        scratch_shapes=[pltpu.VMEM(kv.shape, BF16), pltpu.SemaphoreType.DMA((2,))],
        compiler_params=PARAMS,
        name="prefix_state",
    )(early.astype(jnp.int32).reshape(1), line_queries, kv, early_near, late_near, far_keys, far_values)
    received = exchange(partial, lines)

    weight = out_weight.T
    far_weight = swap(weight, 2)
    weights, far_weights = both(weight), both(far_weight)

    attended = pl.pallas_call(
        combine_kernel,
        out_shape=jax.ShapeDtypeStruct((depth, rows, hd), BF16),
        in_specs=vmem(4),
        out_specs=vmem(1)[0],
        compiler_params=PARAMS,
        name="combine",
    )(received, *own)

    line_rows = exchange(attended, lines)
    columns = weight.shape[0]
    product = pl.pallas_call(
        project_kernel,
        out_shape=jax.ShapeDtypeStruct((4, heads, depth * steps // heads, columns), F32),
        in_specs=[SMEM] + vmem(3),
        out_specs=vmem(1)[0],
        compiler_params=PARAMS,
        name="project",
    )((place % 4).reshape(1), line_rows, weights, far_weights)
    product = product.reshape(4 * heads, depth * steps // heads, columns)
    terms = lax.all_to_all(product, ("ctx", "head"), 0, 0, axis_index_groups=planes, tiled=True)
    return pl.pallas_call(
        finish_kernel,
        out_shape=jax.ShapeDtypeStruct(residual.shape, BF16),
        in_specs=vmem(2),
        out_specs=vmem(1)[0],
        compiler_params=PARAMS,
        name="finish",
    )(terms.reshape(4, heads, depth * steps // heads, columns), residual)


def solution(mesh):
    in_specs = (
        P(None, "ctx", "head", None),
        P(None, "ctx", "head", None),
        P(None, "ctx", "head", None),
        P("ctx", None, "head", None),
        P("ctx", None, "head", None),
        P("ctx"),
        P("ctx", "head", None),
        P("ctx", "head", None),
        P("head", "ctx"),
        P(None, "head", "ctx"),
    )
    out_specs = P(None, "head", "ctx")
    return jax.shard_map(body, mesh=mesh, in_specs=in_specs, out_specs=out_specs, check_vma=False)
```

```python
import functools
import math

import jax
import jax.numpy as jnp
from jax import lax
from jax.experimental import pallas as pl
from jax.experimental.pallas import tpu as pltpu
from jax.sharding import PartitionSpec as P

NEG_FILL = -1e30
BF16, F32 = jnp.bfloat16, jnp.float32
SCALE = math.log2(math.e) / math.sqrt(128)
NT = (((1,), (1,)), ((), ()))
EARLY_Z = 5
LINE_ORDER = [11, 10, 9, 8, 7, 6, 5, 4, 3, 2, 1, 0, 15, 14, 13, 12]
SIDE_ORDER, HEAD_ORDER = [1, 2, 3, 0], [5, 6, 7, 0, 1, 2, 3, 4]


def split_three(x):
    high = x.astype(BF16).astype(F32)
    rest = x - high
    middle = rest.astype(BF16).astype(F32)
    return [high, middle, rest - middle]


def sample_rows(parts, count):
    lanes = 16 * count
    sample = lax.broadcasted_iota(jnp.int32, (count, lanes), 0)
    mine = sample == lax.broadcasted_iota(jnp.int32, (count, lanes), 1) // 16
    stacked = jnp.concatenate([jnp.where(mine, part, 0.0) for part in parts], 0).astype(BF16)
    place = lax.broadcasted_iota(jnp.int32, (lanes, 128), 0) % 16
    fold = (place == lax.broadcasted_iota(jnp.int32, (lanes, 128), 1) % 16).astype(F32).astype(BF16)
    folded = jnp.dot(stacked, fold, preferred_element_type=F32)
    lane_part = lax.broadcasted_iota(jnp.int32, (count, 128), 1) // 16
    rows = jnp.zeros((count, 128), F32)
    for p in range(len(parts)):
        rows = jnp.where(lane_part == p, folded[p * count : (p + 1) * count], rows)
    return rows


def hand_on_kernel(_, out_ref):
    out_ref[...] = jnp.zeros_like(out_ref)


def untouched_kernel(_, out_ref):
    pass


def prefix_kernel(
    early_ref, q_ref, kv_ref, early_near_ref, late_near_ref, fk_ref, fv_ref, out_ref, near_ref, sems
):
    depth = kv_ref.shape[0] // 2
    k_ref, v_ref = kv_ref.at[0:depth], kv_ref.at[depth : 2 * depth]

    def moves(source):
        return [
            pltpu.make_async_copy(source.at[part], near_ref.at[part], sems.at[i])
            for i, part in enumerate((pl.ds(0, depth), pl.ds(depth, depth)))
        ]

    @pl.when(early_ref[0] > 0)
    def _():
        for move in moves(early_near_ref):
            move.start()

    @pl.when(early_ref[0] <= 0)
    def _():
        for move in moves(late_near_ref):
            move.start()

    def arrived():
        @pl.when(early_ref[0] > 0)
        def _():
            for move in moves(early_near_ref):
                move.wait()

        @pl.when(early_ref[0] <= 0)
        def _():
            for move in moves(late_near_ref):
                move.wait()

    prefix_state(q_ref, k_ref, v_ref, near_ref, fk_ref, fv_ref, out_ref, arrived)


def prefix_state(q_ref, k_ref, v_ref, near_ref, fk_ref, fv_ref, out_ref, arrived):
    key_block, row_block = 256, 128
    depth = k_ref.shape[0]
    starts = range(0, depth, key_block)
    shards = [
        (k_ref, v_ref),
        (fk_ref.at[0], fv_ref.at[0]),
        (fk_ref.at[1], fv_ref.at[1]),
        (near_ref.at[0:depth], near_ref.at[depth : 2 * depth]),
    ]
    spans = [slice(at, at + row_block) for at in range(0, q_ref.shape[0], row_block)]
    def score(span, k):
        return [
            lax.dot_general(q_ref[span, :], k[i : i + key_block, :], NT, preferred_element_type=F32) for i in starts
        ]

    held = [[s for k, _ in shards[:-1] for s in score(span, k)] for span in spans]
    arrived()
    all_scores = [scores + score(span, shards[-1][0]) for span, scores in zip(spans, held)]
    values = [v[i : i + key_block, :] for _, v in shards for i in starts]
    for span, scores in zip(spans, all_scores):
        highest = functools.reduce(jnp.maximum, scores).max(1, keepdims=True)
        totals, weighted = [], []
        for s, v in zip(scores, values):
            p = jnp.exp2((s - highest) * SCALE)
            totals.append(p)
            weighted.append(jnp.dot(p.astype(BF16), v, preferred_element_type=F32))
        total = functools.reduce(jnp.add, totals).sum(1, keepdims=True)
        weighted = functools.reduce(jnp.add, weighted)
        first, count = span.start // 16, row_block // 16
        out_ref[first : first + count, 0:8] = weighted.astype(BF16).reshape(count, 8, 2, 128)
        lane = lax.broadcasted_iota(jnp.int32, (row_block, 128), 1)
        stats = jnp.zeros((row_block, 128), F32)
        parts = split_three(highest) + split_three(total)
        for p, part in enumerate(parts):
            stats = jnp.where(lane == p, part, stats)
        stats = stats.T
        rows = sample_rows([stats[p : p + 1] for p in range(len(parts))], count).astype(BF16)
        out_ref[first : first + count, 8] = jnp.broadcast_to(rows[:, None, :], (count, 2, 128))


def suffix_kernel(length_ref, q_ref, sk_ref, sv_ref, nk_ref, nv_ref, o_ref, m_ref, l_ref):
    q = q_ref[...]
    s = lax.dot_general(q, sk_ref[...], NT, preferred_element_type=F32)
    usable = lax.broadcasted_iota(jnp.int32, s.shape, 1) < length_ref[0]
    s = jnp.where(usable, s, NEG_FILL)
    q_wide = q.astype(F32)
    new_keys, new_values = nk_ref[...].astype(F32), nv_ref[...].astype(F32)
    rows = q.shape[0]
    second = lax.broadcasted_iota(jnp.int32, (rows, 1), 0) >= rows // 2
    n0 = (q_wide * new_keys[0:1]).sum(1, keepdims=True)
    n1 = jnp.where(second, (q_wide * new_keys[1:2]).sum(1, keepdims=True), NEG_FILL)
    highest = jnp.maximum(s.max(1, keepdims=True), jnp.maximum(n0, n1))
    p = jnp.where(usable, jnp.exp2((s - highest) * SCALE), 0.0)
    p0 = jnp.exp2((n0 - highest) * SCALE)
    p1 = jnp.where(second, jnp.exp2((n1 - highest) * SCALE), 0.0)
    weighted = jnp.dot(p.astype(BF16), sv_ref[...], preferred_element_type=F32)
    weighted = weighted + p0.astype(BF16).astype(F32) * new_values[0:1] + p1.astype(BF16).astype(F32) * new_values[1:2]
    o_ref[...] = weighted
    m_ref[...] = jnp.broadcast_to(highest, m_ref.shape)
    l_ref[...] = jnp.broadcast_to(p.sum(1, keepdims=True) + p0 + p1, l_ref.shape)


def combine_kernel(got_ref, so_ref, sm_ref, sl_ref, out_ref):
    sources = got_ref.shape[0]
    stats = got_ref[:, 8].astype(F32)[:, 0, :]
    parts = jnp.concatenate([stats, jnp.zeros((128 - sources, 128), F32)], 0).T[:, 0:sources]
    maxima = parts[0:16] + (parts[16:32] + parts[32:48])
    totals = parts[48:64] + (parts[64:80] + parts[80:96])
    own_max, own_total = sm_ref[:, 0:1], sl_ref[:, 0:1]
    top = jnp.maximum(maxima.max(1, keepdims=True), own_max)
    factor = jnp.exp2((maxima - top) * SCALE)
    own_factor = jnp.exp2((own_max - top) * SCALE)
    weight_total = (factor * totals).sum(1, keepdims=True) + own_factor * own_total
    weighted = own_factor * so_ref[...]
    for i in range(sources):
        weighted = weighted + factor[:, i : i + 1] * got_ref[i, 0:8].astype(F32).reshape(16, 128)
    attended = (weighted / weight_total).astype(BF16)
    out_ref[...] = jnp.broadcast_to(attended[None], out_ref.shape)


def project_kernel(place_ref, x_ref, w_ref, far_ref, out_ref):
    samples, rows, hd = x_ref.shape
    group = w_ref.shape[2] // hd
    heads, chunk = out_ref.shape[1:3]
    steps = rows // group
    x = x_ref[...].astype(F32).reshape(samples * steps, group, hd)
    x = jnp.swapaxes(x, 0, 1).astype(BF16)
    side = place_ref[0] // 2 * 2
    for ref, at in ((w_ref, side), (far_ref, 2 - side)):
        for core in range(2):
            y = functools.reduce(
                jnp.add,
                [
                    lax.dot_general(
                        x[g], ref[core, :, g * hd : (g + 1) * hd], NT, preferred_element_type=F32
                    )
                    for g in range(group)
                ],
            )
            to = functools.reduce(jnp.add, [jnp.where(at + core == d, p, 0) for p, d in enumerate(SIDE_ORDER)])
            for member, z in enumerate(LINE_ORDER):
                shard, slot = divmod(z * heads, samples)
                first = slot * chunk // samples
                out_ref[to, HEAD_ORDER.index(shard), first : first + steps] = y[member * steps : (member + 1) * steps]


def finish_kernel(terms_ref, residual_ref, out_ref):
    planes, heads = terms_ref.shape[:2]
    steps = residual_ref.shape[0]
    sums = [
        functools.reduce(jnp.add, [terms_ref[SIDE_ORDER.index(d), h] for h in range(heads)]) for d in range(planes)
    ]
    for t in range(steps):
        rows = [sums[d][z * steps + t][None] for z in range(sums[0].shape[0] // steps) for d in range(planes)]
        out_ref[t] = (jnp.concatenate(rows, 0) + residual_ref[t].astype(F32)).astype(BF16)


def vmem(n):
    return [pl.BlockSpec(memory_space=pltpu.VMEM)] * n


SMEM = pl.BlockSpec(memory_space=pltpu.SMEM)
PARAMS = pltpu.CompilerParams(vmem_limit_bytes=32 * 1024 * 1024)


def body(
    queries,
    new_keys,
    new_values,
    suffix_keys,
    suffix_values,
    suffix_lengths,
    prefix_keys,
    prefix_values,
    out_weight,
    residual,
):
    steps, _, group, hd = queries.shape
    rows = steps * group
    ctx = lax.axis_size("ctx")
    heads = lax.axis_size("head")
    depth = ctx // 4
    lines = [[4 * z + j for z in LINE_ORDER] for j in range(4)]
    halves = [[2 * i + core for i in range(ctx // 2)] for core in range(2)]
    pairs = [[2 * i, 2 * i + 1] for i in range(ctx // 2)]
    planes = [[(4 * z + j) * heads + h for j in SIDE_ORDER for h in HEAD_ORDER] for z in range(depth)]
    place = lax.axis_index("ctx").astype(jnp.int32)

    def swap(x, bit):
        return lax.ppermute(x, "ctx", [(i, i ^ bit) for i in range(ctx)])

    def early_swap(x):
        near = swap(x, 1)
        after = pl.pallas_call(
            hand_on_kernel,
            out_shape=jax.ShapeDtypeStruct((rows, hd), BF16),
            in_specs=[pl.BlockSpec(memory_space=pl.ANY)],
            out_specs=vmem(1)[0],
            compiler_params=PARAMS,
            name="hand_on",
        )(near)
        return near, after

    def untouched(x):
        return pl.pallas_call(
            untouched_kernel,
            out_shape=jax.ShapeDtypeStruct(x.shape, x.dtype),
            in_specs=[pl.BlockSpec(memory_space=pl.ANY)],
            out_specs=pl.BlockSpec(memory_space=pl.ANY),
            compiler_params=PARAMS,
            name="untouched",
        )(x)

    def exchange(x, groups):
        return lax.all_to_all(x, "ctx", 0, 0, axis_index_groups=groups, tiled=True)

    def both(x):
        return lax.all_gather(x, "ctx", axis=0, axis_index_groups=pairs)

    query_rows = queries.reshape(rows, hd)
    kv = jnp.concatenate([prefix_keys.reshape(-1, hd), prefix_values.reshape(-1, hd)], 0)
    far = swap(kv, 2)
    early = place // 4 < EARLY_Z
    early_near, nothing = lax.cond(early, early_swap, lambda x: (untouched(x), jnp.zeros((rows, hd), BF16)), kv)
    copies = jnp.broadcast_to((query_rows + nothing)[None], (depth, rows, hd))
    line_queries = exchange(copies, lines).reshape(depth * rows, hd)
    late_near = lax.cond(early, lambda x: untouched(x), lambda x: swap(x, 1), kv)
    half = kv.shape[0] // 2
    far_keys, far_values = both(far[:half]), both(far[half:])

    own = pl.pallas_call(
        suffix_kernel,
        out_shape=[jax.ShapeDtypeStruct((rows, hd), F32)] * 3,
        in_specs=[SMEM] + vmem(5),
        out_specs=vmem(3),
        compiler_params=PARAMS,
        name="suffix_state",
    )(
        suffix_lengths,
        query_rows,
        suffix_keys.reshape(-1, hd),
        suffix_values.reshape(-1, hd),
        new_keys.reshape(-1, hd),
        new_values.reshape(-1, hd),
    )

    partial = pl.pallas_call(
        prefix_kernel,
        out_shape=jax.ShapeDtypeStruct((depth, rows // 2 + 1, 2, hd), BF16),
        in_specs=[SMEM] + vmem(2) + [pl.BlockSpec(memory_space=pl.ANY)] * 2 + vmem(2),
        out_specs=vmem(1)[0],
        scratch_shapes=[pltpu.VMEM(kv.shape, BF16), pltpu.SemaphoreType.DMA((2,))],
        compiler_params=PARAMS,
        name="prefix_state",
    )(early.astype(jnp.int32).reshape(1), line_queries, kv, early_near, late_near, far_keys, far_values)
    received = exchange(partial, lines)

    weight = out_weight.T
    far_weight = swap(weight, 2)
    weights, far_weights = both(weight), both(far_weight)

    attended = pl.pallas_call(
        combine_kernel,
        out_shape=jax.ShapeDtypeStruct((depth, rows, hd), BF16),
        in_specs=vmem(4),
        out_specs=vmem(1)[0],
        compiler_params=PARAMS,
        name="combine",
    )(received, *own)

    line_rows = exchange(attended, lines)
    columns = weight.shape[0]
    product = pl.pallas_call(
        project_kernel,
        out_shape=jax.ShapeDtypeStruct((4, heads, depth * steps // heads, columns), F32),
        in_specs=[SMEM] + vmem(3),
        out_specs=vmem(1)[0],
        compiler_params=PARAMS,
        name="project",
    )((place % 4).reshape(1), line_rows, weights, far_weights)
    product = product.reshape(4 * heads, depth * steps // heads, columns)
    terms = lax.all_to_all(product, ("ctx", "head"), 0, 0, axis_index_groups=planes, tiled=True)
    return pl.pallas_call(
        finish_kernel,
        out_shape=jax.ShapeDtypeStruct(residual.shape, BF16),
        in_specs=vmem(2),
        out_specs=vmem(1)[0],
        compiler_params=PARAMS,
        name="finish",
    )(terms.reshape(4, heads, depth * steps // heads, columns), residual)


def solution(mesh):
    in_specs = (
        P(None, "ctx", "head", None),
        P(None, "ctx", "head", None),
        P(None, "ctx", "head", None),
        P("ctx", None, "head", None),
        P("ctx", None, "head", None),
        P("ctx"),
        P("ctx", "head", None),
        P("ctx", "head", None),
        P("head", "ctx"),
        P(None, "head", "ctx"),
    )
    out_specs = P(None, "head", "ctx")
    return jax.shard_map(body, mesh=mesh, in_specs=in_specs, out_specs=out_specs, check_vma=False)
```
